128 devices in a mesh: dom: 32 (over z, x, core), sub: 4 (over y).
Axes of the slice: x: 4, y: 4, z: 4, core: 2. Of those that a mesh axis runs over, the one named last changes fastest.
Arguments:
- leaf_mult: bfloat16 [131072, 488], P(('dom', 'sub')), may hold values from -6 to 6
- m2m: bfloat16 [8, 488, 488], replicated, may hold values from -0.09375 to 0.09375
- compress: bfloat16 [488, 128], replicated, may hold values from -0.25 to 0.25
- m2l_core: bfloat16 [316, 128, 128], P('sub'), may hold values from -0.0390625 to 0.0390625
- expand: bfloat16 [128, 488], replicated, may hold values from -0.5 to 0.5
- l2l: bfloat16 [488, 8, 488], replicated, may hold values from -0.25 to 0.25
- inherited: bfloat16 [131072, 488], P(('dom', 'sub')), may hold values from -6 to 6
- send_rows: int32 [32, 32, 32], P('dom'), may hold values from 0 to 511, as said below
- m2l_list: int32 [16384, 316], P('dom', 'sub'), may hold values from -1 to 1535, as said below
Outputs:
- leaf_local: bfloat16 [131072, 488], P(('dom', 'sub'))
The draws below stay inside these ranges and needn't reach their ends.
Inputs may be any that keep to these rules, and one draw needn't show every extreme that they name: Rows of the sending partition; send_rows[0, 1, 0] is 511 and send_rows[0, 1, 1] is 0. A program may pack several of these whole-number row indices into one word while they travel. `m2l_list`: A target of partition p refers to a received slot j from partition s (s != p) only if j < min(32, max(16, 32 >> (|s - p| - 1))); slots of s = p are never referred to.
All inputs are finite; a program needn't handle non-finite values.
Results may differ from the reference program's by a relative error of at most 0.017.
Values may be sent and summed in bfloat16 or wider, within the bound.
No kernel may reach another device: no remote copies, remote signals or barrier semaphores. Data moves between devices by JAX's collectives and lax.ppermute only.
A program may use at most 64 MiB of HBM per device.

```python
import jax
import jax.numpy as jnp
from jax import lax

P_SIZE = 488
RANK = 128
NOFF = 316
KIDS = 8
CAP = 32
NPART = 32
OCT_PART = 512
OCTANTS = 16384
LEAVES = 131072


def draw_send_rows(key, part):
    key = jax.random.fold_in(key, 11)
    rows = jax.random.randint(key, (NPART, NPART, CAP), 0, OCT_PART)
    rows = rows.at[0, 1, 0].set(OCT_PART - 1)
    rows = rows.at[0, 1, 1].set(0)
    return rows.astype(jnp.int32)


def draw_m2l_list(key, part):
    key = jax.random.fold_in(key, 12)
    keys = jax.random.split(key, 5)
    shape = (OCTANTS, NOFF)
    target_part = (jnp.arange(OCTANTS, dtype=jnp.int32) // OCT_PART)[:, None]
    present = jax.random.randint(keys[0], shape, 0, 5) < 3
    remote = jax.random.randint(keys[1], shape, 0, 2) == 1
    local_row = jax.random.randint(keys[2], shape, 0, OCT_PART)
    other = jax.random.randint(keys[3], shape, 0, NPART - 1)
    source = other + (other >= target_part).astype(jnp.int32)
    distance = jnp.abs(source - target_part)
    count = jnp.maximum(16, jnp.right_shift(jnp.full(shape, CAP, jnp.int32), distance - 1))
    count = jnp.minimum(count, CAP)
    slot = jax.random.randint(keys[4], shape, 0, count)
    remote_row = OCT_PART + source * CAP + slot
    value = jnp.where(present, jnp.where(remote, remote_row, local_row), -1)
    value = value.at[(NPART - 2) * OCT_PART, 0].set(OCT_PART + NPART * CAP - 1)
    value = value.at[0, 1].set(-1)
    return value.astype(jnp.int32)


def block_scale(stream_key, dims, cuts, smallest, top_value):
    loudness, own = 1.0, jax.random.fold_in(stream_key, 6)
    for position, shards_of in cuts:
        steps = jnp.exp(jax.random.uniform(jax.random.fold_in(own, position), (shards_of,), jnp.float32, smallest / len(cuts), top_value / len(cuts)))
        loudness = loudness * jnp.repeat(steps, dims[position] // shards_of).reshape([-1 if axis == position else 1 for axis in range(len(dims))])
    return loudness


def gaussian(rng, dims, deviation, bound, cuts=(), kind=jnp.bfloat16):
    level = block_scale(rng, dims, cuts, -0.22, 0.18) if cuts else 1.0
    values = jax.random.normal(rng, dims, jnp.float32) * deviation * level
    return jnp.minimum(jnp.maximum(values, -bound), bound).astype(kind)


def setup_inputs(seed: int = 0) -> dict:
    streams_of = jax.random.split(jax.random.key(seed), 10)
    return {
        "leaf_mult": gaussian(streams_of[0], (LEAVES, P_SIZE), 1.0, 6.0, ((0, 128),)),
        "m2m": gaussian(streams_of[1], (KIDS, P_SIZE, P_SIZE), (KIDS * P_SIZE) ** -0.5, 0.09375),
        "compress": gaussian(streams_of[2], (P_SIZE, RANK), P_SIZE ** -0.5, 0.25),
        "m2l_core": gaussian(streams_of[3], (NOFF, RANK, RANK), (NOFF * RANK * 3 // 5) ** -0.5, 0.0390625, ((0, 4),)),
        "expand": gaussian(streams_of[4], (RANK, P_SIZE), RANK ** -0.5, 0.5),
        "l2l": gaussian(streams_of[5], (P_SIZE, KIDS, P_SIZE), P_SIZE ** -0.5, 0.25),
        "inherited": gaussian(streams_of[6], (LEAVES, P_SIZE), 1.0, 6.0, ((0, 128),)),
        "send_rows": draw_send_rows(jax.random.fold_in(streams_of[9], 71), 0),
        "m2l_list": draw_m2l_list(jax.random.fold_in(streams_of[9], 71), 0),
    }


def reference(leaf_mult, m2m, compress, m2l_core, expand, l2l, inherited, send_rows, m2l_list):
    kids_flat = leaf_mult.reshape(OCTANTS, KIDS * P_SIZE)
    parents = jnp.dot(kids_flat, m2m.reshape(KIDS * P_SIZE, P_SIZE), preferred_element_type=jnp.float32).astype(jnp.bfloat16)
    packed = jnp.dot(parents, compress, preferred_element_type=jnp.float32).astype(jnp.bfloat16)
    core_flat = m2l_core.reshape(NOFF * RANK, RANK)
    sources = jnp.arange(NPART, dtype=jnp.int32)

    def one_part(index):
        index = index.astype(jnp.int32)
        own = lax.dynamic_slice_in_dim(packed, index * OCT_PART, OCT_PART, 0)
        wanted = jnp.take(send_rows, index, axis=1)
        global_rows = (sources[:, None] * OCT_PART + wanted).reshape(-1).astype(jnp.int32)
        table = jnp.concatenate([own, jnp.take(packed, global_rows, axis=0)], axis=0)
        listed = lax.dynamic_slice_in_dim(m2l_list, index * OCT_PART, OCT_PART, 0)
        picked = jnp.take(table, jnp.maximum(listed, 0).reshape(-1), axis=0).reshape(OCT_PART, NOFF, RANK)
        picked = picked * (listed >= 0).astype(picked.dtype)[:, :, None]
        return jnp.dot(picked.reshape(OCT_PART, NOFF * RANK), core_flat, preferred_element_type=jnp.float32)

    acc = lax.map(one_part, sources).reshape(OCTANTS, RANK)
    acc_low = acc.astype(jnp.bfloat16)
    parent_local = jnp.dot(acc_low, expand, preferred_element_type=jnp.float32).astype(jnp.bfloat16)
    children = jnp.dot(parent_local, l2l.reshape(P_SIZE, KIDS * P_SIZE), preferred_element_type=jnp.float32)
    result = children.reshape(LEAVES, P_SIZE) + inherited.astype(jnp.float32)
    return result.astype(jnp.bfloat16)
```

```python
import jax
import jax.numpy as jnp
from jax import lax
from jax.experimental import pallas as pl
from jax.experimental.pallas import tpu as pltpu
from jax.sharding import PartitionSpec as P

BF = jnp.bfloat16
F32 = jnp.float32
I32 = jnp.int32
MIB = 1 << 20
CAP = 32
SURE = 16
NONE = 1023

VMEM = pl.BlockSpec(memory_space=pltpu.VMEM)
ANY = pl.BlockSpec(memory_space=pl.ANY)


def dot(a, b):
    return jnp.dot(a, b, preferred_element_type=F32)


def call(kernel, name, out, ins, scratch, limit, flops, nbytes):
    return pl.pallas_call(
        kernel,
        name=name,
        out_shape=out,
        in_specs=ins,
        out_specs=jax.tree.map(lambda _: VMEM, out),
        scratch_shapes=scratch,
        compiler_params=pltpu.CompilerParams(vmem_limit_bytes=limit * MIB),
        cost_estimate=pl.CostEstimate(flops=flops, bytes_accessed=nbytes, transcendentals=0),
    )


def strided(ref, first, count, stride, width):
    parts = [ref[i, pl.ds(first, count, stride=stride), :] for i in range(ref.shape[0])]
    return jnp.concatenate(parts, axis=1)[:, :width].astype(BF)


def up_kernel(leaf_ref, m2m_ref, compress_ref, out_ref, rows_ref, m2m_buf, sems):
    nkids, width = m2m_ref.shape[0], m2m_ref.shape[1]
    count = leaf_ref.shape[1] // nkids
    copies = [
        pltpu.make_async_copy(m2m_ref.at[c], m2m_buf.at[c], sems.at[c]) for c in range(nkids)
    ]
    for copy in copies:
        copy.start()
    for j in range(leaf_ref.shape[1] // 128):
        cols = slice(j * 128, (j + 1) * 128)
        for i, base in enumerate(range(0, width, 128)):
            size = min(128, width - base)
            rows_ref[i, cols, :size] = leaf_ref[base:base + size, cols].astype(F32).T
    total = jnp.zeros((count, width), F32)
    for c in range(nkids):
        kid = strided(rows_ref, c, count, nkids, width)
        copies[c].wait()
        total = total + dot(kid, m2m_buf[c])
    out_ref[...] = dot(total.astype(BF), compress_ref[...]).astype(BF)


def upward(leaf_t, m2m, compress):
    nkids, width, _ = m2m.shape
    count = leaf_t.shape[1] // nkids
    return call(
        up_kernel,
        "upward",
        jax.ShapeDtypeStruct((count, compress.shape[1]), BF),
        [VMEM, ANY, VMEM],
        [
            pltpu.VMEM((-(-width // 128), leaf_t.shape[1], 128), F32),
            pltpu.VMEM(m2m.shape, BF),
            pltpu.SemaphoreType.DMA((nkids,)),
        ],
        24,
        2 * leaf_t.size * width,
        2 * (leaf_t.size + m2m.size),
    )(leaf_t, m2m, compress)


def pick_kernel(own_ref, one_ref, two_ref, three_ref, rows_ref, part_ref, send_ref):
    me = lax.axis_index("sub")
    count = own_ref.shape[0]
    for shift, ref in enumerate((own_ref, one_ref, two_ref, three_ref)):
        start = lax.rem(me + (4 - shift), 4) * count
        part_ref[pl.ds(pl.multiple_of(start, count), count), :] = ref[...]
    part = part_ref[...]
    wanted = rows_ref.shape[0]
    rows = jnp.broadcast_to(rows_ref[...], (wanted, 128)).astype(jnp.int16)
    lane = lax.broadcasted_iota(I32, (1, 128), 1)
    hot = jnp.concatenate(
        [
            jnp.where(rows == (lane + base).astype(jnp.int16), BF(1), BF(0))
            for base in range(0, part.shape[0], 128)
        ],
        axis=1,
    )
    send_ref[...] = dot(hot, part).astype(BF).reshape(send_ref.shape)


def pick(pieces, rows, npart):
    count, rank = pieces[0].shape
    return call(
        pick_kernel,
        "pick",
        (
            jax.ShapeDtypeStruct((4 * count, rank), BF),
            jax.ShapeDtypeStruct((npart, CAP, rank), BF),
        ),
        [VMEM] * 5,
        [],
        16,
        2 * rows.shape[0] * 4 * count * rank,
        2 * rows.shape[0] * rank,
    )(*pieces, rows)


def prep_kernel(list_ref, code_ref, extra_ref):
    part = lax.axis_index("dom")
    offsets, count = list_ref.shape
    value = list_ref[...]
    remote = value - count
    source = lax.shift_right_arithmetic(remote, 5)
    slot = remote & (CAP - 1)
    sure = slot < SURE
    below = source < part
    row = jnp.where(sure, source * SURE + slot, part * SURE + slot - SURE)
    far = jnp.where(sure | below, row + 1024, NONE)
    code = jnp.where(value < 0, NONE, jnp.where(value < count, value, far))
    extra = jnp.where((value >= count) & (slot >= SURE) & (source > part), slot - SURE, -1)
    pad = jnp.full((128 - offsets, count), -1, I32)
    code = jnp.concatenate([code, pad], axis=0)
    extra = jnp.concatenate([extra, pad], axis=0)
    for j in range(count // 128):
        cols = slice(j * 128, (j + 1) * 128)
        code_ref[cols, :] = code[:, cols].T
        extra_ref[cols, :] = extra[:, cols].astype(F32).T.astype(BF)


def prepare(list_t):
    offsets, count = list_t.shape
    return call(
        prep_kernel,
        "prepare",
        (jax.ShapeDtypeStruct((count, 128), I32), jax.ShapeDtypeStruct((count, 128), BF)),
        [VMEM],
        [],
        16,
        1,
        4 * list_t.size,
    )(list_t)


def split_kernel(l2l_ref, out_ref, wide_ref):
    width, nkids, _ = l2l_ref.shape
    for i, base in enumerate(range(0, width, 128)):
        size = min(128, width - base)
        block = l2l_ref[:, :, base:base + size].astype(F32)
        wide_ref[i, :, :size] = block.reshape(width * nkids, size)
    for c in range(nkids):
        out_ref[c] = strided(wide_ref, c, width, nkids, width)


def split(l2l):
    width, nkids, _ = l2l.shape
    return call(
        split_kernel,
        "split",
        jax.ShapeDtypeStruct((nkids, width, width), BF),
        [VMEM],
        [pltpu.VMEM((-(-width // 128), width * nkids, 128), F32)],
        24,
        1,
        4 * l2l.size,
    )(l2l)


def m2l_kernel(code_ref, extra_ref, part_ref, got_ref, core_ref, *rest):
    outs, (table_ref, acc_ref, z_ref) = rest[:4], rest[4:]
    here, me = lax.axis_index("dom"), lax.axis_index("sub")
    count, rank = part_ref.shape
    npart = got_ref.shape[0]
    offsets = core_ref.shape[0]
    table_ref[:, :rank] = part_ref[...]
    table_ref[:, rank:] = got_ref[:, :SURE, :].reshape(npart * SURE, rank)
    low = got_ref[pl.ds(jnp.maximum(here - 1, 0), 1), SURE:, :].reshape(SURE, rank)
    table_ref[pl.ds(pl.multiple_of(here * SURE, SURE), SURE), rank:] = low
    high = got_ref[pl.ds(jnp.minimum(here + 1, npart - 1), 1), SURE:, :].reshape(SURE, rank)
    none = jnp.zeros_like(high)
    tail = jnp.concatenate(
        [jnp.concatenate([high, none], axis=1), jnp.concatenate([none, high], axis=1)], axis=0
    )
    table = table_ref[...]
    lane = lax.broadcasted_iota(I32, (1, 128), 1)
    for k in range(0, offsets, 2):
        ks = range(k, min(k + 2, offsets))
        picked = []
        for kk in ks:
            code = jnp.broadcast_to(code_ref[:, kk:kk + 1], (count, 128))
            row = (code & 1023).astype(jnp.int16)
            hot = jnp.concatenate(
                [
                    jnp.where(row == (lane + base).astype(jnp.int16), BF(1), BF(0))
                    for base in range(0, count, 128)
                ],
                axis=1,
            )
            both = dot(hot, table)
            picked.append(jnp.where(code >= 1024, both[:, rank:], both[:, :rank]).astype(BF))
        n = len(picked)
        lhs = jnp.concatenate(
            [jnp.concatenate(picked, axis=1), tail[:n * SURE, :n * rank]], axis=0
        )
        both = dot(lhs, core_ref[k:k + n].reshape(n * rank, rank))
        z_ref[k * SURE:(k + n) * SURE, :] = both[count:].astype(BF)
        if k == 0:
            acc_ref[...] = both[:count]
        else:
            acc_ref[...] += both[:count]
    zrows = z_ref.shape[0]
    if zrows > offsets * SURE:
        z_ref[offsets * SURE:, :] = jnp.zeros((zrows - offsets * SURE, rank), BF)
    ahead = lax.broadcasted_iota(I32, (128, zrows), 0)
    group = lax.shift_right_logical(lax.broadcasted_iota(I32, (128, zrows), 1), 4)
    spread = dot(extra_ref[...], jnp.where(ahead == group, 1.0, 0.0).astype(BF))
    slot = (lax.broadcasted_iota(I32, (1, zrows), 1) & (SURE - 1)).astype(F32)
    hot = jnp.where(spread == slot, 1.0, 0.0).astype(BF)
    acc_ref[...] += dot(hot, z_ref[...])
    share = count // 4
    for shift, out in enumerate(outs):
        start = lax.rem(me + shift, 4) * share
        out[...] = acc_ref[pl.ds(pl.multiple_of(start, share), share), :].astype(out.dtype)


def m2l(code, extra, part, got, core):
    count, rank = part.shape
    offsets = core.shape[0]
    zrows = -(-offsets * SURE // 128) * 128
    piece = (count // 4, rank)
    return call(
        m2l_kernel,
        "m2l",
        tuple(jax.ShapeDtypeStruct(piece, BF if i else F32) for i in range(4)),
        [VMEM] * 5,
        [
            pltpu.VMEM((count, 2 * rank), BF),
            pltpu.VMEM((count, rank), F32),
            pltpu.VMEM((zrows, rank), BF),
        ],
        32,
        2 * count * offsets * rank * (2 * count + rank),
        2 * core.size,
    )(code, extra, part, got, core)


def down_kernel(own_ref, one_ref, two_ref, three_ref, expand_ref, l2l_ref, inh_ref, out_ref, rows_ref):
    nkids, width = l2l_ref.shape[0], l2l_ref.shape[1]
    count = own_ref.shape[0]
    acc = own_ref[...]
    for ref in (one_ref, two_ref, three_ref):
        acc = acc + ref[...].astype(F32)
    local = lax.dot_general(
        acc.astype(BF), expand_ref[...], (((1,), (1,)), ((), ())), preferred_element_type=F32
    ).astype(BF)
    for c in range(nkids):
        kid = dot(local, l2l_ref[c])
        kid = jnp.concatenate([kid, jnp.zeros((count, -width % 128), F32)], axis=1)
        for i in range(rows_ref.shape[0]):
            rows_ref[i, pl.ds(c, count, stride=nkids), :] = kid[:, i * 128:(i + 1) * 128]
    for j in range(out_ref.shape[1] // 128):
        cols = slice(j * 128, (j + 1) * 128)
        for i, base in enumerate(range(0, width, 128)):
            rows = slice(base, min(base + 128, width))
            far = rows_ref[i, cols, :].T[:rows.stop - base]
            out_ref[rows, cols] = (far + inh_ref[rows, cols].astype(F32)).astype(BF)


def downward(pieces, expand_t, l2l, inherited_t):
    nkids, width, _ = l2l.shape
    return call(
        down_kernel,
        "downward",
        jax.ShapeDtypeStruct(inherited_t.shape, BF),
        [VMEM] * 7,
        [pltpu.VMEM((-(-width // 128), inherited_t.shape[1], 128), F32)],
        32,
        2 * inherited_t.size * width,
        2 * (2 * inherited_t.size + l2l.size),
    )(*pieces, expand_t, l2l, inherited_t)


def local(leaf_mult, m2m, compress, m2l_core, expand, l2l, inherited, send_rows, m2l_list):
    npart, nsub = lax.axis_size("dom"), lax.axis_size("sub")

    def shifted(x, shift):
        return lax.ppermute(x, "sub", [(i, (i + shift) % nsub) for i in range(nsub)])

    packed = upward(leaf_mult.T, m2m, compress)
    pieces = [packed] + [shifted(packed, shift) for shift in (1, 2, 3)]
    code, extra = prepare(m2l_list.T)
    kids = split(l2l)
    part, send = pick(pieces, send_rows.reshape(npart * CAP, 1), npart)
    got = lax.all_to_all(send, "dom", 0, 0, tiled=True)
    sums = m2l(code, extra, part, got, m2l_core)
    sums = [sums[0]] + [shifted(sums[shift], shift) for shift in (1, 2, 3)]
    return downward(sums, expand.T, kids, inherited.T).T


def solution(mesh):
    placed = (
        P(("dom", "sub"), None),
        P(),
        P(),
        P("sub", None, None),
        P(),
        P(),
        P(("dom", "sub"), None),
        P("dom", None, None),
        P("dom", "sub"),
    )
    return jax.shard_map(
        local, mesh=mesh, in_specs=placed, out_specs=P(("dom", "sub"), None), check_vma=False
    )
```

```python
import jax
import jax.numpy as jnp
from jax import lax
from jax.experimental import pallas as pl
from jax.experimental.pallas import tpu as pltpu
from jax.sharding import PartitionSpec as P

BF = jnp.bfloat16
F32 = jnp.float32
I32 = jnp.int32
I16 = jnp.int16
MIB = 1 << 20
CAP = 32
SURE = 16
STEP = 2
HALF = 256

VMEM = pl.BlockSpec(memory_space=pltpu.VMEM)
HBM = pl.BlockSpec(memory_space=pltpu.HBM)


def dot(a, b):
    return jnp.dot(a, b, preferred_element_type=F32)


def call(kernel, name, out, ins, scratch, limit, flops, nbytes, place=VMEM):
    return pl.pallas_call(
        kernel,
        name=name,
        out_shape=out,
        in_specs=ins,
        out_specs=jax.tree.map(lambda _: place, out),
        scratch_shapes=scratch,
        compiler_params=pltpu.CompilerParams(vmem_limit_bytes=limit * MIB),
        cost_estimate=pl.CostEstimate(flops=flops, bytes_accessed=nbytes, transcendentals=0),
    )


def strided(ref, first, count, stride, width):
    parts = [ref[i, pl.ds(first, count, stride=stride), :] for i in range(ref.shape[0])]
    return jnp.concatenate(parts, axis=1)[:, :width].astype(BF)


def up_kernel(leaf_ref, m2m_ref, compress_ref, out_ref, leaf_buf, m2m_buf, compress_buf, rows_ref, sems):
    nkids, width = m2m_ref.shape[0], m2m_ref.shape[1]
    count = leaf_ref.shape[1] // nkids
    first = pltpu.make_async_copy(leaf_ref, leaf_buf, sems.at[nkids])
    copies = [
        pltpu.make_async_copy(m2m_ref.at[c], m2m_buf.at[c], sems.at[c]) for c in range(nkids)
    ]
    last = pltpu.make_async_copy(compress_ref, compress_buf, sems.at[nkids + 1])
    first.start()
    for copy in copies:
        copy.start()
    last.start()
    first.wait()
    for j in range(leaf_ref.shape[1] // 128):
        cols = slice(j * 128, (j + 1) * 128)
        for i, base in enumerate(range(0, width, 128)):
            size = min(128, width - base)
            rows_ref[i, cols, :size] = leaf_buf[base:base + size, cols].astype(F32).T
    total = jnp.zeros((count, width), F32)
    for c in range(nkids):
        kid = strided(rows_ref, c, count, nkids, width)
        copies[c].wait()
        total = total + dot(kid, m2m_buf[c])
    last.wait()
    out_ref[...] = dot(total.astype(BF), compress_buf[...]).astype(BF)


def upward(leaf_t, m2m, compress):
    nkids, width, _ = m2m.shape
    count = leaf_t.shape[1] // nkids
    return call(
        up_kernel,
        "upward",
        jax.ShapeDtypeStruct((count, compress.shape[1]), BF),
        [HBM] * 3,
        [
            pltpu.VMEM(leaf_t.shape, BF),
            pltpu.VMEM(m2m.shape, BF),
            pltpu.VMEM(compress.shape, BF),
            pltpu.VMEM((-(-width // 128), leaf_t.shape[1], 128), F32),
            pltpu.SemaphoreType.DMA((nkids + 2,)),
        ],
        60,
        2 * leaf_t.size * width,
        2 * (leaf_t.size + m2m.size),
    )(leaf_t, m2m, compress)


def one_hot(row, depth, first=0):
    lane = lax.broadcasted_iota(I32, (1, 128), 1)
    return jnp.concatenate(
        [
            jnp.where(row == (lane + (first + base)).astype(I16), BF(1), BF(0))
            for base in range(0, depth, 128)
        ],
        axis=1,
    )


def prep_kernel(list_ref, rows_ref, packed_ref, code_ref, hot_ref, own_ref):
    own_ref[...] = packed_ref[...]
    part = lax.axis_index("dom")
    offsets, count = list_ref.shape
    wanted = rows_ref.shape[0]
    hot_ref[...] = one_hot(jnp.broadcast_to(rows_ref[...], (wanted, 128)).astype(I16), count)
    value = list_ref[...]
    source = lax.shift_right_arithmetic(value - count, 5)
    slot = value & (CAP - 1)
    sure = slot < SURE
    row = jnp.where(sure, source * SURE + slot, part * SURE + slot - SURE)
    extra = ~sure & (source > part)
    code = jnp.where(extra, slot + (2 * count - SURE), row + count)
    code = jnp.where(value < count, value, code)
    code = jnp.concatenate([code, jnp.full((128 - offsets, count), -1, I32)], axis=0)
    for j in range(count // 128):
        cols = slice(j * 128, (j + 1) * 128)
        code_ref[cols, :] = code[:, cols].T.astype(I16)


def prepare(list_t, rows, packed):
    count = list_t.shape[1]
    return call(
        prep_kernel,
        "prepare",
        (
            jax.ShapeDtypeStruct((count, 128), I16),
            jax.ShapeDtypeStruct((rows.shape[0], count), BF),
            jax.ShapeDtypeStruct(packed.shape, BF),
        ),
        [VMEM] * 3,
        [],
        16,
        1,
        4 * list_t.size,
    )(list_t, rows, packed)


def pick_kernel(own_ref, one_ref, two_ref, three_ref, hot_ref, part_ref, send_ref):
    me = lax.axis_index("sub")
    count = own_ref.shape[0]
    for shift, ref in enumerate((own_ref, one_ref, two_ref, three_ref)):
        start = lax.rem(me + (4 - shift), 4) * count
        part_ref[pl.ds(pl.multiple_of(start, count), count), :] = ref[...]
    send_ref[...] = dot(hot_ref[...], part_ref[...]).astype(BF).reshape(send_ref.shape)


def pick(pieces, hot, npart):
    count, rank = pieces[0].shape
    return call(
        pick_kernel,
        "pick",
        (
            jax.ShapeDtypeStruct((4 * count, rank), BF),
            jax.ShapeDtypeStruct((npart, CAP, rank), BF),
        ),
        [VMEM] * 5,
        [],
        16,
        2 * hot.size * rank,
        2 * hot.size,
    )(*pieces, hot)


def split_kernel(l2l_ref, out_ref, wide_ref):
    width, nkids, _ = l2l_ref.shape
    for i, base in enumerate(range(0, width, 128)):
        size = min(128, width - base)
        block = l2l_ref[:, :, base:base + size].astype(F32)
        wide_ref[i, :, :size] = block.reshape(width * nkids, size)
    for c in range(nkids):
        out_ref[c] = strided(wide_ref, c, width, nkids, width)


def split(l2l):
    width, nkids, _ = l2l.shape
    return call(
        split_kernel,
        "split",
        jax.ShapeDtypeStruct((nkids, width, width), BF),
        [VMEM],
        [pltpu.VMEM((-(-width // 128), width * nkids, 128), F32)],
        24,
        1,
        4 * l2l.size,
    )(l2l)


def either(test, both):
    rank = both.shape[1] // 2
    return jnp.where(test != 0, both[:, rank:].astype(BF), both[:, :rank].astype(BF))


def accumulate(wide_ref, first, table_ref, core_ref, acc_ref):
    offsets, rank = core_ref.shape[0], core_ref.shape[1]
    table = table_ref[...]
    for k in range(0, offsets, STEP):
        n = min(STEP, offsets - k)
        lhs = []
        for i in range(k, k + n):
            code = jnp.broadcast_to(wide_ref[:, i:i + 1], wide_ref.shape).astype(I16)
            both = dot(one_hot(code & I16(~HALF), HALF, first), table)
            lhs.append(either(code & I16(HALF), both))
        core = core_ref[k:k + n].reshape(n * rank, rank)
        acc_ref[...] += dot(jnp.concatenate(lhs, axis=1), core)


def near_kernel(code_ref, part_ref, core_ref, acc_ref, table_ref, wide_ref):
    wide_ref[...] = code_ref[...].astype(I32)
    rank = part_ref.shape[1]
    table_ref[:, :rank] = part_ref[:HALF, :]
    table_ref[:, rank:] = part_ref[HALF:, :]
    acc_ref[...] = jnp.zeros_like(acc_ref)
    accumulate(wide_ref, 0, table_ref, core_ref, acc_ref)


def near(code, part, core):
    count, rank = part.shape
    return call(
        near_kernel,
        "near",
        jax.ShapeDtypeStruct((count, rank), F32),
        [VMEM] * 3,
        [pltpu.VMEM((HALF, 2 * rank), BF), pltpu.VMEM(code.shape, I32)],
        24,
        2 * count * core.shape[0] * rank * (count + rank),
        2 * core.size,
    )(code, part, core)


def far_kernel(code_ref, near_ref, got_ref, core_ref, *rest):
    outs, (table_ref, wide_ref, acc_ref, z_ref) = rest[:4], rest[4:]
    wide_ref[...] = code_ref[...].astype(I32)
    here, me = lax.axis_index("dom"), lax.axis_index("sub")
    npart, _, rank = got_ref.shape
    offsets = core_ref.shape[0]
    cut = npart // 2
    table_ref[:, :rank] = got_ref[:cut, :SURE, :].reshape(HALF, rank)
    table_ref[:, rank:] = got_ref[cut:, :SURE, :].reshape(HALF, rank)
    low = got_ref[pl.ds(jnp.maximum(here - 1, 0), 1), SURE:, :].reshape(SURE, rank)
    spot = pl.ds(pl.multiple_of(lax.rem(here, cut) * SURE, SURE), SURE)
    table_ref[spot, :rank] = jnp.where(here < cut, low, table_ref[spot, :rank])
    table_ref[spot, rank:] = jnp.where(here < cut, table_ref[spot, rank:], low)
    high = got_ref[pl.ds(jnp.minimum(here + 1, npart - 1), 1), SURE:, :].reshape(SURE, rank)
    none = jnp.zeros_like(high)
    tail = jnp.concatenate(
        [
            jnp.concatenate([none] * i + [high] + [none] * (STEP - 1 - i), axis=1)
            for i in range(STEP)
        ],
        axis=0,
    )
    zrows = z_ref.shape[0]
    z_ref[offsets * SURE:, :] = jnp.zeros((zrows - offsets * SURE, rank), BF)
    for k in range(0, offsets, STEP):
        n = min(STEP, offsets - k)
        core = core_ref[k:k + n].reshape(n * rank, rank)
        z_ref[k * SURE:(k + n) * SURE, :] = dot(tail[:n * SURE, :n * rank], core).astype(BF)
    slot = (lax.broadcasted_iota(I32, (1, zrows), 1) & (SURE - 1)).astype(F32) + 1.0
    ahead = lax.broadcasted_iota(I32, (128, zrows), 0)
    group = lax.shift_right_logical(lax.broadcasted_iota(I32, (128, zrows), 1), 4)
    spread = jnp.where(ahead == group, 1.0, 0.0).astype(BF)
    extra = jnp.maximum(wide_ref[...] - (4 * HALF - 1), 0).astype(F32).astype(BF)
    hot = jnp.where(dot(extra, spread) == slot, 1.0, 0.0).astype(BF)
    acc_ref[...] = near_ref[...] + dot(hot, z_ref[...])
    accumulate(wide_ref, 2 * HALF, table_ref, core_ref, acc_ref)
    share = acc_ref.shape[0] // 4
    for shift, out in enumerate(outs):
        start = lax.rem(me + shift, 4) * share
        out[...] = acc_ref[pl.ds(pl.multiple_of(start, share), share), :].astype(out.dtype)


def far(code, near_sums, got, core):
    count, rank = near_sums.shape
    offsets = core.shape[0]
    zrows = (offsets * SURE // 128 + 1) * 128
    piece = (count // 4, rank)
    return call(
        far_kernel,
        "far",
        tuple(jax.ShapeDtypeStruct(piece, BF if i else F32) for i in range(4)),
        [VMEM] * 4,
        [
            pltpu.VMEM((HALF, 2 * rank), BF),
            pltpu.VMEM(code.shape, I32),
            pltpu.VMEM((count, rank), F32),
            pltpu.VMEM((zrows, rank), BF),
        ],
        24,
        2 * count * offsets * rank * (count + rank),
        2 * core.size,
    )(code, near_sums, got, core)


def down_kernel(own_ref, one_ref, two_ref, three_ref, expand_ref, l2l_ref, inh_ref, out_ref, rows_ref):
    nkids, width = l2l_ref.shape[0], l2l_ref.shape[1]
    count = own_ref.shape[0]
    acc = own_ref[...]
    for ref in (one_ref, two_ref, three_ref):
        acc = acc + ref[...].astype(F32)
    local = lax.dot_general(
        acc.astype(BF), expand_ref[...], (((1,), (1,)), ((), ())), preferred_element_type=F32
    ).astype(BF)
    for c in range(nkids):
        kid = dot(local, l2l_ref[c])
        kid = jnp.concatenate([kid, jnp.zeros((count, -width % 128), F32)], axis=1)
        for i in range(rows_ref.shape[0]):
            rows_ref[i, pl.ds(c, count, stride=nkids), :] = kid[:, i * 128:(i + 1) * 128]
    for j in range(out_ref.shape[1] // 128):
        cols = slice(j * 128, (j + 1) * 128)
        for i, base in enumerate(range(0, width, 128)):
            rows = slice(base, min(base + 128, width))
            far = rows_ref[i, cols, :].T[:rows.stop - base]
            out_ref[rows, cols] = (far + inh_ref[rows, cols].astype(F32)).astype(BF)


def downward(pieces, expand_t, l2l, inherited_t):
    nkids, width, _ = l2l.shape
    return call(
        down_kernel,
        "downward",
        jax.ShapeDtypeStruct(inherited_t.shape, BF),
        [VMEM] * 7,
        [pltpu.VMEM((-(-width // 128), inherited_t.shape[1], 128), F32)],
        32,
        2 * inherited_t.size * width,
        2 * (2 * inherited_t.size + l2l.size),
    )(*pieces, expand_t, l2l, inherited_t)


def local(leaf_mult, m2m, compress, m2l_core, expand, l2l, inherited, send_rows, m2l_list):
    npart, nsub = lax.axis_size("dom"), lax.axis_size("sub")

    def shifted(x, shift):
        return lax.ppermute(x, "sub", [(i, (i + shift) % nsub) for i in range(nsub)])

    packed = upward(leaf_mult.T, m2m, compress)
    moved = [shifted(packed, shift) for shift in (1, 2, 3)]
    code, hot, own = prepare(m2l_list.T, send_rows.reshape(npart * CAP, 1), packed)
    kids = split(l2l)
    part, send = pick([own] + moved, hot, npart)
    got = lax.all_to_all(send, "dom", 0, 0, tiled=True)
    near_sums = near(code, part, m2l_core)
    sums = far(code, near_sums, got, m2l_core)
    sums = [sums[0]] + [shifted(sums[shift], shift) for shift in (1, 2, 3)]
    return downward(sums, expand.T, kids, inherited.T).T


def solution(mesh):
    placed = (
        P(("dom", "sub"), None),
        P(),
        P(),
        P("sub", None, None),
        P(),
        P(),
        P(("dom", "sub"), None),
        P("dom", None, None),
        P("dom", "sub"),
    )
    return jax.shard_map(
        local, mesh=mesh, in_specs=placed, out_specs=P(("dom", "sub"), None), check_vma=False
    )
```

```python
import jax
import jax.numpy as jnp
from jax import lax
from jax.experimental import pallas as pl
from jax.experimental.pallas import tpu as pltpu
from jax.sharding import PartitionSpec as P

BF = jnp.bfloat16
F32 = jnp.float32
I32 = jnp.int32
I16 = jnp.int16
MIB = 1 << 20
CAP = 32
SURE = 16
STEP = 4
HALF = 256
PITCH = 9

VMEM = pl.BlockSpec(memory_space=pltpu.VMEM)
HBM = pl.BlockSpec(memory_space=pltpu.HBM)


def dot(a, b):
    return jnp.dot(a, b, preferred_element_type=F32)


def call(kernel, name, out, ins, scratch, limit, flops, nbytes, place=VMEM):
    return pl.pallas_call(
        kernel,
        name=name,
        out_shape=out,
        in_specs=ins,
        out_specs=jax.tree.map(lambda _: place, out),
        scratch_shapes=scratch,
        compiler_params=pltpu.CompilerParams(vmem_limit_bytes=limit * MIB),
        cost_estimate=pl.CostEstimate(flops=flops, bytes_accessed=nbytes, transcendentals=0),
    )


def kid_rows(ref, kid, count, width):
    parts = [ref[i, pl.ds(kid, count, stride=PITCH), :] for i in range(ref.shape[0])]
    return jnp.concatenate(parts, axis=1)[:, :width].astype(BF)


def up_kernel(leaf_ref, m2m_ref, compress_ref, out_ref, leaf_buf, m2m_buf, compress_buf, rows_ref, sems):
    nkids, width = m2m_ref.shape[0], m2m_ref.shape[1]
    count = leaf_ref.shape[1] // nkids
    first = pltpu.make_async_copy(leaf_ref, leaf_buf, sems.at[nkids])
    copies = [
        pltpu.make_async_copy(m2m_ref.at[c], m2m_buf.at[c], sems.at[c]) for c in range(nkids)
    ]
    last = pltpu.make_async_copy(compress_ref, compress_buf, sems.at[nkids + 1])
    first.start()
    for copy in copies:
        copy.start()
    last.start()
    first.wait()
    for j in range(leaf_ref.shape[1] // 128):
        cols = slice(j * 128, (j + 1) * 128)
        for i, base in enumerate(range(0, width, 128)):
            size = min(128, width - base)
            turned = leaf_buf[base:base + size, cols].astype(F32).T
            for o in range(0, 128, nkids):
                at = (j * 128 + o) // nkids * PITCH
                rows_ref[i, at:at + nkids, :size] = turned[o:o + nkids]
    total = jnp.zeros((count, width), F32)
    for c in range(nkids):
        kid = kid_rows(rows_ref, c, count, width)
        copies[c].wait()
        total = total + dot(kid, m2m_buf[c])
    last.wait()
    out_ref[...] = dot(total.astype(BF), compress_buf[...]).astype(BF)


def upward(leaf_t, m2m, compress):
    nkids, width, _ = m2m.shape
    count = leaf_t.shape[1] // nkids
    return call(
        up_kernel,
        "upward",
        jax.ShapeDtypeStruct((count, compress.shape[1]), BF),
        [HBM] * 3,
        [
            pltpu.VMEM(leaf_t.shape, BF),
            pltpu.VMEM(m2m.shape, BF),
            pltpu.VMEM(compress.shape, BF),
            pltpu.VMEM((-(-width // 128), count * PITCH, 128), F32),
            pltpu.SemaphoreType.DMA((nkids + 2,)),
        ],
        60,
        2 * leaf_t.size * width,
        2 * (leaf_t.size + m2m.size),
    )(leaf_t, m2m, compress)


def one_hot(row, depth, first=0):
    lane = lax.broadcasted_iota(I32, (1, 128), 1)
    return jnp.concatenate(
        [
            jnp.where(row == (lane + (first + base)).astype(I16), BF(1), BF(0))
            for base in range(0, depth, 128)
        ],
        axis=1,
    )


def prep_kernel(list_ref, rows_ref, packed_ref, code_ref, hot_ref, own_ref):
    own_ref[...] = packed_ref[...]
    part = lax.axis_index("dom")
    offsets, count = list_ref.shape
    wanted = rows_ref.shape[0]
    hot_ref[...] = one_hot(jnp.broadcast_to(rows_ref[...], (wanted, 128)).astype(I16), count)
    value = list_ref[...]
    source = lax.shift_right_arithmetic(value - count, 5)
    slot = value & (CAP - 1)
    sure = slot < SURE
    row = jnp.where(sure, source * SURE + slot, part * SURE + slot - SURE)
    extra = ~sure & (source > part)
    code = jnp.where(extra, slot + (2 * count - SURE), row + count)
    code = jnp.where(value < count, value, code)
    code = jnp.concatenate([code, jnp.full((128 - offsets, count), -1, I32)], axis=0)
    for j in range(count // 128):
        cols = slice(j * 128, (j + 1) * 128)
        code_ref[cols, :] = code[:, cols].T.astype(I16)


def prepare(list_t, rows, packed):
    count = list_t.shape[1]
    return call(
        prep_kernel,
        "prepare",
        (
            jax.ShapeDtypeStruct((count, 128), I16),
            jax.ShapeDtypeStruct((rows.shape[0], count), BF),
            jax.ShapeDtypeStruct(packed.shape, BF),
        ),
        [VMEM] * 3,
        [],
        16,
        1,
        4 * list_t.size,
    )(list_t, rows, packed)


def pick_kernel(own_ref, one_ref, two_ref, three_ref, hot_ref, part_ref, send_ref):
    me = lax.axis_index("sub")
    count = own_ref.shape[0]
    for shift, ref in enumerate((own_ref, one_ref, two_ref, three_ref)):
        start = lax.rem(me + (4 - shift), 4) * count
        part_ref[pl.ds(pl.multiple_of(start, count), count), :] = ref[...]
    send_ref[...] = dot(hot_ref[...], part_ref[...]).astype(BF).reshape(send_ref.shape)


def pick(pieces, hot, npart):
    count, rank = pieces[0].shape
    return call(
        pick_kernel,
        "pick",
        (
            jax.ShapeDtypeStruct((4 * count, rank), BF),
            jax.ShapeDtypeStruct((npart, CAP, rank), BF),
        ),
        [VMEM] * 5,
        [],
        16,
        2 * hot.size * rank,
        2 * hot.size,
    )(*pieces, hot)


def split_kernel(l2l_ref, out_ref, wide_ref):
    width, nkids, _ = l2l_ref.shape
    for i, base in enumerate(range(0, width, 128)):
        size = min(128, width - base)
        block = l2l_ref[:, :, base:base + size].astype(F32)
        for p in range(width):
            wide_ref[i, p * PITCH:p * PITCH + nkids, :size] = block[p]
    for c in range(nkids):
        out_ref[c] = kid_rows(wide_ref, c, width, width)


def split(l2l):
    width, nkids, _ = l2l.shape
    return call(
        split_kernel,
        "split",
        jax.ShapeDtypeStruct((nkids, width, width), BF),
        [VMEM],
        [pltpu.VMEM((-(-width // 128), width * PITCH, 128), F32)],
        24,
        1,
        4 * l2l.size,
    )(l2l)


def either(test, both):
    rank = both.shape[1] // 2
    return jnp.where(test != 0, both[:, rank:].astype(BF), both[:, :rank].astype(BF))


def accumulate(wide_ref, first, table_ref, core_ref, acc_ref, z_ref=None):
    offsets, rank = core_ref.shape[0], core_ref.shape[1]
    table = table_ref[...]
    lane = lax.broadcasted_iota(I32, (1, 128), 1)
    owner = lax.shift_right_logical(lane, 4).astype(I16)
    wanted = ((lane & (SURE - 1)) + 4 * HALF).astype(I16)
    per = 128 // SURE
    mixed, hots = None, []
    for k in range(0, offsets, STEP):
        n = min(STEP, offsets - k)
        lhs = []
        for i in range(k, k + n):
            code = jnp.broadcast_to(wide_ref[:, i:i + 1], wide_ref.shape).astype(I16)
            both = dot(one_hot(code & I16(~HALF), HALF, first), table)
            lhs.append(either(code & I16(HALF), both))
            if z_ref is None:
                continue
            mixed = code if i % per == 0 else jnp.where(owner == I16(i % per), code, mixed)
            if i % per == per - 1 or i == offsets - 1:
                hots.append(jnp.where(mixed == wanted, BF(1), BF(0)))
        core = core_ref[k:k + n].reshape(n * rank, rank)
        acc_ref[...] += dot(jnp.concatenate(lhs, axis=1), core)
        if len(hots) == 2 or (hots and k + n == offsets):
            rows = pl.ds((k + n - 1) // (2 * per) * 256, 128 * len(hots))
            acc_ref[...] += dot(jnp.concatenate(hots, axis=1), z_ref[rows, :])
            hots = []


def near_kernel(code_ref, part_ref, core_ref, acc_ref, table_ref, wide_ref):
    wide_ref[...] = code_ref[...].astype(I32)
    rank = part_ref.shape[1]
    table_ref[:, :rank] = part_ref[:HALF, :]
    table_ref[:, rank:] = part_ref[HALF:, :]
    acc_ref[...] = jnp.zeros_like(acc_ref)
    accumulate(wide_ref, 0, table_ref, core_ref, acc_ref)


def near(code, part, core):
    count, rank = part.shape
    return call(
        near_kernel,
        "near",
        jax.ShapeDtypeStruct((count, rank), F32),
        [VMEM] * 3,
        [pltpu.VMEM((HALF, 2 * rank), BF), pltpu.VMEM(code.shape, I32)],
        24,
        2 * count * core.shape[0] * rank * (count + rank),
        2 * core.size,
    )(code, part, core)


def far_kernel(code_ref, near_ref, got_ref, core_ref, *rest):
    outs, (table_ref, wide_ref, acc_ref, z_ref) = rest[:4], rest[4:]
    wide_ref[...] = code_ref[...].astype(I32)
    here, me = lax.axis_index("dom"), lax.axis_index("sub")
    npart, _, rank = got_ref.shape
    offsets = core_ref.shape[0]
    cut = npart // 2
    table_ref[:, :rank] = got_ref[:cut, :SURE, :].reshape(HALF, rank)
    table_ref[:, rank:] = got_ref[cut:, :SURE, :].reshape(HALF, rank)
    low = got_ref[pl.ds(jnp.maximum(here - 1, 0), 1), SURE:, :].reshape(SURE, rank)
    spot = pl.ds(pl.multiple_of(lax.rem(here, cut) * SURE, SURE), SURE)
    table_ref[spot, :rank] = jnp.where(here < cut, low, table_ref[spot, :rank])
    table_ref[spot, rank:] = jnp.where(here < cut, table_ref[spot, rank:], low)
    high = got_ref[pl.ds(jnp.minimum(here + 1, npart - 1), 1), SURE:, :].reshape(SURE, rank)
    none = jnp.zeros_like(high)
    tail = jnp.concatenate(
        [
            jnp.concatenate([none] * i + [high] + [none] * (STEP - 1 - i), axis=1)
            for i in range(STEP)
        ],
        axis=0,
    )
    zrows = z_ref.shape[0]
    z_ref[offsets * SURE:, :] = jnp.zeros((zrows - offsets * SURE, rank), BF)
    for k in range(0, offsets, STEP):
        n = min(STEP, offsets - k)
        core = core_ref[k:k + n].reshape(n * rank, rank)
        z_ref[k * SURE:(k + n) * SURE, :] = dot(tail[:n * SURE, :n * rank], core).astype(BF)
    acc_ref[...] = near_ref[...]
    accumulate(wide_ref, 2 * HALF, table_ref, core_ref, acc_ref, z_ref)
    share = acc_ref.shape[0] // 4
    for shift, out in enumerate(outs):
        start = lax.rem(me + shift, 4) * share
        out[...] = acc_ref[pl.ds(pl.multiple_of(start, share), share), :].astype(out.dtype)


def far(code, near_sums, got, core):
    count, rank = near_sums.shape
    offsets = core.shape[0]
    zrows = (offsets * SURE // 128 + 1) * 128
    piece = (count // 4, rank)
    return call(
        far_kernel,
        "far",
        tuple(jax.ShapeDtypeStruct(piece, BF if i else F32) for i in range(4)),
        [VMEM] * 4,
        [
            pltpu.VMEM((HALF, 2 * rank), BF),
            pltpu.VMEM(code.shape, I32),
            pltpu.VMEM((count, rank), F32),
            pltpu.VMEM((zrows, rank), BF),
        ],
        24,
        2 * count * offsets * rank * (count + rank),
        2 * core.size,
    )(code, near_sums, got, core)


def down_kernel(own_ref, one_ref, two_ref, three_ref, expand_ref, l2l_ref, inh_ref, out_hbm, rows_ref, out_ref, sems):
    nkids, width = l2l_ref.shape[0], l2l_ref.shape[1]
    count = own_ref.shape[0]
    acc = own_ref[...]
    for ref in (one_ref, two_ref, three_ref):
        acc = acc + ref[...].astype(F32)
    local = lax.dot_general(
        acc.astype(BF), expand_ref[...], (((1,), (1,)), ((), ())), preferred_element_type=F32
    ).astype(BF)
    for c in range(nkids):
        kid = dot(local, l2l_ref[c])
        kid = jnp.concatenate([kid, jnp.zeros((count, -width % 128), F32)], axis=1)
        for i in range(rows_ref.shape[0]):
            rows_ref[i, pl.ds(c, count, stride=PITCH), :] = kid[:, i * 128:(i + 1) * 128]
    copies = []
    for i, base in enumerate(range(0, width, 128)):
        rows = slice(base, min(base + 128, width))
        for j in range(out_ref.shape[1] // 128):
            cols = slice(j * 128, (j + 1) * 128)
            first = j * 128 // nkids
            far = jnp.concatenate(
                [
                    rows_ref[i, o * PITCH:o * PITCH + nkids, :]
                    for o in range(first, first + 128 // nkids)
                ],
                axis=0,
            ).T[:rows.stop - base]
            out_ref[rows, cols] = (far + inh_ref[rows, cols].astype(F32)).astype(BF)
        part = pl.ds(base, rows.stop - base)
        copies.append(pltpu.make_async_copy(out_ref.at[part], out_hbm.at[part], sems.at[i]))
        copies[-1].start()
    for copy in copies:
        copy.wait()


def downward(pieces, expand_t, l2l, inherited_t):
    nkids, width, _ = l2l.shape
    blocks = -(-width // 128)
    return call(
        down_kernel,
        "downward",
        jax.ShapeDtypeStruct(inherited_t.shape, BF),
        [VMEM] * 7,
        [
            pltpu.VMEM((blocks, pieces[0].shape[0] * PITCH, 128), F32),
            pltpu.VMEM(inherited_t.shape, BF),
            pltpu.SemaphoreType.DMA((blocks,)),
        ],
        32,
        2 * inherited_t.size * width,
        2 * (2 * inherited_t.size + l2l.size),
        HBM,
    )(*pieces, expand_t, l2l, inherited_t)


def local(leaf_mult, m2m, compress, m2l_core, expand, l2l, inherited, send_rows, m2l_list):
    npart, nsub = lax.axis_size("dom"), lax.axis_size("sub")

    def shifted(x, shift):
        return lax.ppermute(x, "sub", [(i, (i + shift) % nsub) for i in range(nsub)])

    packed = upward(leaf_mult.T, m2m, compress)
    moved = [shifted(packed, shift) for shift in (1, 2, 3)]
    code, hot, own = prepare(m2l_list.T, send_rows.reshape(npart * CAP, 1), packed)
    kids = split(l2l)
    part, send = pick([own] + moved, hot, npart)
    got = lax.all_to_all(send, "dom", 0, 0, tiled=True)
    near_sums = near(code, part, m2l_core)
    sums = far(code, near_sums, got, m2l_core)
    sums = [sums[0]] + [shifted(sums[shift], shift) for shift in (1, 2, 3)]
    return downward(sums, expand.T, kids, inherited.T).T


def solution(mesh):
    placed = (
        P(("dom", "sub"), None),
        P(),
        P(),
        P("sub", None, None),
        P(),
        P(),
        P(("dom", "sub"), None),
        P("dom", None, None),
        P("dom", "sub"),
    )
    return jax.shard_map(
        local, mesh=mesh, in_specs=placed, out_specs=P(("dom", "sub"), None), check_vma=False
    )
```

```python
import functools

import jax
import jax.numpy as jnp
from jax import lax
from jax.experimental import pallas as pl
from jax.experimental.pallas import tpu as pltpu
from jax.sharding import PartitionSpec as P

BF = jnp.bfloat16
F32 = jnp.float32
I32 = jnp.int32
I16 = jnp.int16
MIB = 1 << 20
CAP = 32
SURE = 16
STEP = 4
HALF = 256
PITCH = 9

VMEM = pl.BlockSpec(memory_space=pltpu.VMEM)
HBM = pl.BlockSpec(memory_space=pltpu.HBM)


def dot(a, b):
    return jnp.dot(a, b, preferred_element_type=F32)


def call(kernel, name, out, ins, scratch, limit, flops, nbytes):
    return pl.pallas_call(
        kernel,
        name=name,
        out_shape=out,
        in_specs=ins,
        out_specs=jax.tree.map(lambda _: VMEM, out),
        scratch_shapes=scratch,
        compiler_params=pltpu.CompilerParams(vmem_limit_bytes=limit * MIB),
        cost_estimate=pl.CostEstimate(flops=flops, bytes_accessed=nbytes, transcendentals=0),
    )


def kid_rows(ref, kid, count, width):
    parts = [ref[i, pl.ds(kid, count, stride=PITCH), :] for i in range(ref.shape[0])]
    return jnp.concatenate(parts, axis=1)[:, :width].astype(BF)


def up_kernel(leaf_ref, m2m_ref, compress_ref, out_ref, leaf_buf, m2m_buf, compress_buf, rows_ref, sems):
    nkids, width = m2m_ref.shape[0], m2m_ref.shape[1]
    count = leaf_ref.shape[1] // nkids
    first = pltpu.make_async_copy(leaf_ref, leaf_buf, sems.at[nkids])
    copies = [
        pltpu.make_async_copy(m2m_ref.at[c], m2m_buf.at[c], sems.at[c]) for c in range(nkids)
    ]
    last = pltpu.make_async_copy(compress_ref, compress_buf, sems.at[nkids + 1])
    first.start()
    for copy in copies:
        copy.start()
    last.start()
    first.wait()
    for j in range(leaf_ref.shape[1] // 128):
        cols = slice(j * 128, (j + 1) * 128)
        for i, base in enumerate(range(0, width, 128)):
            size = min(128, width - base)
            turned = leaf_buf[base:base + size, cols].astype(F32).T
            for o in range(0, 128, nkids):
                at = (j * 128 + o) // nkids * PITCH
                rows_ref[i, at:at + nkids, :size] = turned[o:o + nkids]
    total = jnp.zeros((count, width), F32)
    for c in range(nkids):
        kid = kid_rows(rows_ref, c, count, width)
        copies[c].wait()
        total = total + dot(kid, m2m_buf[c])
    last.wait()
    out_ref[...] = dot(total.astype(BF), compress_buf[...]).astype(BF)


def upward(leaf_t, m2m, compress):
    nkids, width, _ = m2m.shape
    count = leaf_t.shape[1] // nkids
    return call(
        up_kernel,
        "upward",
        jax.ShapeDtypeStruct((count, compress.shape[1]), BF),
        [HBM] * 3,
        [
            pltpu.VMEM(leaf_t.shape, BF),
            pltpu.VMEM(m2m.shape, BF),
            pltpu.VMEM(compress.shape, BF),
            pltpu.VMEM((-(-width // 128), (count + 2) * PITCH, 128), F32),
            pltpu.SemaphoreType.DMA((nkids + 2,)),
        ],
        60,
        2 * leaf_t.size * width,
        2 * (leaf_t.size + m2m.size),
    )(leaf_t, m2m, compress)


def one_hot(row, depth, first=0):
    lane = lax.broadcasted_iota(I32, (1, 128), 1)
    return jnp.concatenate(
        [
            jnp.where(row == (lane + (first + base)).astype(I16), BF(1), BF(0))
            for base in range(0, depth, 128)
        ],
        axis=1,
    )


def prep_kernel(list_ref, rows_ref, packed_ref, code_ref, hot_ref, own_ref):
    own_ref[...] = packed_ref[...]
    part = lax.axis_index("dom")
    offsets, count = list_ref.shape
    wanted = rows_ref.shape[0]
    hot_ref[...] = one_hot(jnp.broadcast_to(rows_ref[...], (wanted, 128)).astype(I16), count)
    value = list_ref[...]
    source = lax.shift_right_arithmetic(value - count, 5)
    slot = value & (CAP - 1)
    sure = slot < SURE
    row = jnp.where(sure, source * SURE + slot, part * SURE + slot - SURE)
    extra = ~sure & (source > part)
    code = jnp.where(extra, slot + (2 * count - SURE), row + count)
    code = jnp.where(value < count, value, code)
    code = jnp.concatenate([code, jnp.full((128 - offsets, count), -1, I32)], axis=0)
    for j in range(count // 128):
        cols = slice(j * 128, (j + 1) * 128)
        code_ref[cols, :] = code[:, cols].T.astype(I16)


def prepare(list_t, rows, packed):
    count = list_t.shape[1]
    return call(
        prep_kernel,
        "prepare",
        (
            jax.ShapeDtypeStruct((count, 128), I16),
            jax.ShapeDtypeStruct((rows.shape[0], count), BF),
            jax.ShapeDtypeStruct(packed.shape, BF),
        ),
        [VMEM] * 3,
        [],
        16,
        1,
        4 * list_t.size,
    )(list_t, rows, packed)


def pick_kernel(own_ref, one_ref, two_ref, three_ref, hot_ref, part_ref, send_ref):
    me = lax.axis_index("sub")
    count = own_ref.shape[0]
    for shift, ref in enumerate((own_ref, one_ref, two_ref, three_ref)):
        start = lax.rem(me + (4 - shift), 4) * count
        part_ref[pl.ds(pl.multiple_of(start, count), count), :] = ref[...]
    send_ref[...] = dot(hot_ref[...], part_ref[...]).astype(BF).reshape(send_ref.shape)


def pick(pieces, hot, npart):
    count, rank = pieces[0].shape
    return call(
        pick_kernel,
        "pick",
        (
            jax.ShapeDtypeStruct((4 * count, rank), BF),
            jax.ShapeDtypeStruct((npart, CAP, rank), BF),
        ),
        [VMEM] * 5,
        [],
        16,
        2 * hot.size * rank,
        2 * hot.size,
    )(*pieces, hot)


def fold_kernel(expand_ref, l2l_ref, out_ref, wide_ref):
    width, nkids, _ = l2l_ref.shape
    expand = expand_ref[...].astype(F32).T.astype(BF)
    for i, base in enumerate(range(0, width, 128)):
        size = min(128, width - base)
        block = l2l_ref[:, :, base:base + size].astype(F32)
        for p in range(width):
            wide_ref[i, p * PITCH:p * PITCH + nkids, :size] = block[p]
    for c in range(nkids):
        out_ref[c] = dot(expand, kid_rows(wide_ref, c, width, width)).astype(BF)


def fold(expand_t, l2l):
    width, nkids, _ = l2l.shape
    rank = expand_t.shape[1]
    return call(
        fold_kernel,
        "fold",
        jax.ShapeDtypeStruct((nkids, rank, width), BF),
        [VMEM] * 2,
        [pltpu.VMEM((-(-width // 128), (width + 2) * PITCH, 128), F32)],
        24,
        2 * rank * l2l.size,
        2 * l2l.size,
    )(expand_t, l2l)


def either(test, both):
    rank = both.shape[1] // 2
    return jnp.where(test != 0, both[:, rank:].astype(BF), both[:, :rank].astype(BF))


def accumulate(wide_ref, first, table_ref, core_ref, acc_ref, z_ref=None):
    offsets, rank = core_ref.shape[0], core_ref.shape[1]
    table = table_ref[...]
    lane = lax.broadcasted_iota(I32, (1, 128), 1)
    owner = lax.shift_right_logical(lane, 4).astype(I16)
    wanted = ((lane & (SURE - 1)) + 4 * HALF).astype(I16)
    per = 128 // SURE
    mixed, hots = None, []
    for k in range(0, offsets, STEP):
        n = min(STEP, offsets - k)
        lhs = []
        for i in range(k, k + n):
            code = jnp.broadcast_to(wide_ref[:, i:i + 1], wide_ref.shape).astype(I16)
            both = dot(one_hot(code & I16(~HALF), HALF, first), table)
            lhs.append(either(code & I16(HALF), both))
            if z_ref is None:
                continue
            mixed = code if i % per == 0 else jnp.where(owner == I16(i % per), code, mixed)
            if i % per == per - 1 or i == offsets - 1:
                hots.append(jnp.where(mixed == wanted, BF(1), BF(0)))
        core = core_ref[k:k + n].reshape(n * rank, rank)
        acc_ref[...] += dot(jnp.concatenate(lhs, axis=1), core)
        if len(hots) == 2 or (hots and k + n == offsets):
            rows = pl.ds((k + n - 1) // (2 * per) * 256, 128 * len(hots))
            acc_ref[...] += dot(jnp.concatenate(hots, axis=1), z_ref[rows, :])
            hots = []


def widen(code_ref, wide_ref, shifts):
    share = code_ref.shape[0] // 4
    for i, shift in enumerate(shifts):
        start = lax.rem(lax.axis_index("sub") + shift, 4) * share
        rows = code_ref[pl.ds(pl.multiple_of(start, share), share), :]
        wide_ref[i * share:(i + 1) * share, :] = rows.astype(I32)


def near_kernel(code_ref, part_ref, core_ref, acc_ref, table_ref, wide_ref):
    widen(code_ref, wide_ref, range(4))
    rank = part_ref.shape[1]
    table_ref[:, :rank] = part_ref[:HALF, :]
    table_ref[:, rank:] = part_ref[HALF:, :]
    acc_ref[...] = jnp.zeros_like(acc_ref)
    accumulate(wide_ref, 0, table_ref, core_ref, acc_ref)


def near(code, part, core):
    count, rank = part.shape
    return call(
        near_kernel,
        "near",
        jax.ShapeDtypeStruct((count, rank), F32),
        [VMEM] * 3,
        [pltpu.VMEM((HALF, 2 * rank), BF), pltpu.VMEM(code.shape, I32)],
        24,
        2 * count * core.shape[0] * rank * (count + rank),
        2 * core.size,
    )(code, part, core)


def far_kernel(shifts, code_ref, near_ref, got_ref, core_ref, *rest):
    outs, (table_ref, wide_ref, acc_ref, z_ref) = rest[:len(shifts)], rest[len(shifts):]
    widen(code_ref, wide_ref, shifts)
    here = lax.axis_index("dom")
    npart, _, rank = got_ref.shape
    offsets = core_ref.shape[0]
    cut = npart // 2
    table_ref[:, :rank] = got_ref[:cut, :SURE, :].reshape(HALF, rank)
    table_ref[:, rank:] = got_ref[cut:, :SURE, :].reshape(HALF, rank)
    low = got_ref[pl.ds(jnp.maximum(here - 1, 0), 1), SURE:, :].reshape(SURE, rank)
    spot = pl.ds(pl.multiple_of(lax.rem(here, cut) * SURE, SURE), SURE)
    table_ref[spot, :rank] = jnp.where(here < cut, low, table_ref[spot, :rank])
    table_ref[spot, rank:] = jnp.where(here < cut, table_ref[spot, rank:], low)
    high = got_ref[pl.ds(jnp.minimum(here + 1, npart - 1), 1), SURE:, :].reshape(SURE, rank)
    none = jnp.zeros_like(high)
    tail = jnp.concatenate(
        [
            jnp.concatenate([none] * i + [high] + [none] * (STEP - 1 - i), axis=1)
            for i in range(STEP)
        ],
        axis=0,
    )
    zrows = z_ref.shape[0]
    z_ref[offsets * SURE:, :] = jnp.zeros((zrows - offsets * SURE, rank), BF)
    for k in range(0, offsets, STEP):
        n = min(STEP, offsets - k)
        core = core_ref[k:k + n].reshape(n * rank, rank)
        z_ref[k * SURE:(k + n) * SURE, :] = dot(tail[:n * SURE, :n * rank], core).astype(BF)
    share = code_ref.shape[0] // 4
    for i, shift in enumerate(shifts):
        acc_ref[i * share:(i + 1) * share, :] = near_ref[shift * share:(shift + 1) * share, :]
    accumulate(wide_ref, 2 * HALF, table_ref, core_ref, acc_ref, z_ref)
    for i, out in enumerate(outs):
        out[...] = acc_ref[i * share:(i + 1) * share, :].astype(out.dtype)


def far(code, near_sums, got, core, shifts):
    rank = near_sums.shape[1]
    share = near_sums.shape[0] // 4
    count = share * len(shifts)
    offsets = core.shape[0]
    zrows = (offsets * SURE // 128 + 1) * 128
    return call(
        functools.partial(far_kernel, shifts),
        "far",
        tuple(jax.ShapeDtypeStruct((share, rank), BF if shift else F32) for shift in shifts),
        [VMEM] * 4,
        [
            pltpu.VMEM((HALF, 2 * rank), BF),
            pltpu.VMEM((count, 128), I32),
            pltpu.VMEM((count, rank), F32),
            pltpu.VMEM((zrows, rank), BF),
        ],
        24,
        2 * count * offsets * rank * (4 * share + rank),
        2 * core.size,
    )(code, near_sums, got, core)


def down_kernel(own_ref, one_ref, two_ref, three_ref, fold_ref, inh_ref, out_ref, rows_ref):
    nkids, _, width = fold_ref.shape
    count = own_ref.shape[0]
    acc = own_ref[...]
    for ref in (one_ref, two_ref, three_ref):
        acc = acc + ref[...].astype(F32)
    acc = acc.astype(BF)
    for c in range(nkids):
        kid = dot(acc, fold_ref[c])
        kid = jnp.concatenate([kid, jnp.zeros((count, -width % 128), F32)], axis=1)
        for i in range(rows_ref.shape[0]):
            rows_ref[i, pl.ds(c, count, stride=PITCH), :] = kid[:, i * 128:(i + 1) * 128]
    for i, base in enumerate(range(0, width, 128)):
        rows = slice(base, min(base + 128, width))
        for j in range(out_ref.shape[1] // 128):
            cols = slice(j * 128, (j + 1) * 128)
            first = j * 128 // nkids
            far = jnp.concatenate(
                [
                    rows_ref[i, o * PITCH:o * PITCH + nkids, :]
                    for o in range(first, first + 128 // nkids)
                ],
                axis=0,
            ).T[:rows.stop - base]
            out_ref[rows, cols] = (far + inh_ref[rows, cols].astype(F32)).astype(BF)


def downward(pieces, folded, inherited_t):
    nkids, rank, width = folded.shape
    blocks = -(-width // 128)
    return call(
        down_kernel,
        "downward",
        jax.ShapeDtypeStruct(inherited_t.shape, BF),
        [VMEM] * 6,
        [pltpu.VMEM((blocks, (pieces[0].shape[0] + 2) * PITCH, 128), F32)],
        32,
        2 * inherited_t.size * rank,
        2 * (2 * inherited_t.size + folded.size),
    )(*pieces, folded, inherited_t)


def local(leaf_mult, m2m, compress, m2l_core, expand, l2l, inherited, send_rows, m2l_list):
    npart, nsub = lax.axis_size("dom"), lax.axis_size("sub")

    def shifted(x, shift):
        return lax.ppermute(x, "sub", [(i, (i + shift) % nsub) for i in range(nsub)])

    packed = upward(leaf_mult.T, m2m, compress)
    moved = [shifted(packed, shift) for shift in (1, 2, 3)]
    code, hot, own = prepare(m2l_list.T, send_rows.reshape(npart * CAP, 1), packed)
    folded = fold(expand.T, l2l)
    part, send = pick([own] + moved, hot, npart)
    got = lax.all_to_all(send, "dom", 0, 0, tiled=True)
    near_sums = near(code, part, m2l_core)
    sums = far(code, near_sums, got, m2l_core, (0, 1, 2, 3))
    sums = [sums[0]] + [shifted(sums[shift], shift) for shift in (1, 2, 3)]
    return downward(sums, folded, inherited.T).T


def solution(mesh):
    placed = (
        P(("dom", "sub"), None),
        P(),
        P(),
        P("sub", None, None),
        P(),
        P(),
        P(("dom", "sub"), None),
        P("dom", None, None),
        P("dom", "sub"),
    )
    return jax.shard_map(
        local, mesh=mesh, in_specs=placed, out_specs=P(("dom", "sub"), None), check_vma=False
    )
```

```python
import functools

import jax
import jax.numpy as jnp
from jax import lax
from jax.experimental import pallas as pl
from jax.experimental.pallas import tpu as pltpu
from jax.sharding import PartitionSpec as P

BF = jnp.bfloat16
F32 = jnp.float32
I32 = jnp.int32
I16 = jnp.int16
MIB = 1 << 20
CAP = 32
SURE = 16
STEP = 4
HALF = 256
PITCH = 9

VMEM = pl.BlockSpec(memory_space=pltpu.VMEM)
HBM = pl.BlockSpec(memory_space=pltpu.HBM)


def dot(a, b):
    return jnp.dot(a, b, preferred_element_type=F32)


def call(kernel, name, out, ins, scratch, limit, flops, nbytes):
    return pl.pallas_call(
        kernel,
        name=name,
        out_shape=out,
        in_specs=ins,
        out_specs=jax.tree.map(lambda _: VMEM, out),
        scratch_shapes=scratch,
        compiler_params=pltpu.CompilerParams(vmem_limit_bytes=limit * MIB),
        cost_estimate=pl.CostEstimate(flops=flops, bytes_accessed=nbytes, transcendentals=0),
    )


def kid_rows(ref, kid, count, width):
    parts = [ref[i, pl.ds(kid, count, stride=PITCH), :] for i in range(ref.shape[0])]
    return jnp.concatenate(parts, axis=1)[:, :width].astype(BF)


def up_kernel(leaf_ref, m2m_ref, compress_ref, out_ref, leaf_buf, m2m_buf, compress_buf, rows_ref, sems):
    nkids, width = m2m_ref.shape[0], m2m_ref.shape[1]
    count = leaf_ref.shape[1] // nkids
    first = pltpu.make_async_copy(leaf_ref, leaf_buf, sems.at[nkids])
    copies = [
        pltpu.make_async_copy(m2m_ref.at[c], m2m_buf.at[c], sems.at[c]) for c in range(nkids)
    ]
    last = pltpu.make_async_copy(compress_ref, compress_buf, sems.at[nkids + 1])
    first.start()
    for copy in copies:
        copy.start()
    last.start()
    first.wait()
    for j in range(leaf_ref.shape[1] // 128):
        cols = slice(j * 128, (j + 1) * 128)
        for i, base in enumerate(range(0, width, 128)):
            size = min(128, width - base)
            turned = leaf_buf[base:base + size, cols].astype(F32).T
            for o in range(0, 128, nkids):
                at = (j * 128 + o) // nkids * PITCH
                rows_ref[i, at:at + nkids, :size] = turned[o:o + nkids]
    total = jnp.zeros((count, width), F32)
    for c in range(nkids):
        kid = kid_rows(rows_ref, c, count, width)
        copies[c].wait()
        total = total + dot(kid, m2m_buf[c])
    last.wait()
    out_ref[...] = dot(total.astype(BF), compress_buf[...]).astype(BF)


def upward(leaf_t, m2m, compress):
    nkids, width, _ = m2m.shape
    count = leaf_t.shape[1] // nkids
    return call(
        up_kernel,
        "upward",
        jax.ShapeDtypeStruct((count, compress.shape[1]), BF),
        [HBM] * 3,
        [
            pltpu.VMEM(leaf_t.shape, BF),
            pltpu.VMEM(m2m.shape, BF),
            pltpu.VMEM(compress.shape, BF),
            pltpu.VMEM((-(-width // 128), (count + 2) * PITCH, 128), F32),
            pltpu.SemaphoreType.DMA((nkids + 2,)),
        ],
        60,
        2 * leaf_t.size * width,
        2 * (leaf_t.size + m2m.size),
    )(leaf_t, m2m, compress)


def one_hot(row, depth, first=0):
    lane = lax.broadcasted_iota(I32, (1, 128), 1)
    return jnp.concatenate(
        [
            jnp.where(row == (lane + (first + base)).astype(I16), BF(1), BF(0))
            for base in range(0, depth, 128)
        ],
        axis=1,
    )


def prep_kernel(list_ref, rows_ref, packed_ref, code_ref, hot_ref, own_ref):
    own_ref[...] = packed_ref[...]
    part = lax.axis_index("dom")
    offsets, count = list_ref.shape
    wanted = rows_ref.shape[0]
    hot_ref[...] = one_hot(jnp.broadcast_to(rows_ref[...], (wanted, 128)).astype(I16), count)
    value = list_ref[...]
    source = lax.shift_right_arithmetic(value - count, 5)
    slot = value & (CAP - 1)
    sure = slot < SURE
    row = jnp.where(sure, source * SURE + slot, part * SURE + slot - SURE)
    extra = ~sure & (source > part)
    code = jnp.where(extra, slot + (2 * count - SURE), row + count)
    code = jnp.where(value < count, value, code)
    code = jnp.concatenate([code, jnp.full((128 - offsets, count), -1, I32)], axis=0)
    for j in range(count // 128):
        cols = slice(j * 128, (j + 1) * 128)
        code_ref[cols, :] = code[:, cols].T.astype(I16)


def prepare(list_t, rows, packed):
    count = list_t.shape[1]
    return call(
        prep_kernel,
        "prepare",
        (
            jax.ShapeDtypeStruct((count, 128), I16),
            jax.ShapeDtypeStruct((rows.shape[0], count), BF),
            jax.ShapeDtypeStruct(packed.shape, BF),
        ),
        [VMEM] * 3,
        [],
        16,
        1,
        4 * list_t.size,
    )(list_t, rows, packed)


def pick_kernel(own_ref, one_ref, two_ref, three_ref, hot_ref, part_ref, send_ref):
    me = lax.axis_index("sub")
    count = own_ref.shape[0]
    for shift, ref in enumerate((own_ref, one_ref, two_ref, three_ref)):
        start = lax.rem(me + (4 - shift), 4) * count
        part_ref[pl.ds(pl.multiple_of(start, count), count), :] = ref[...]
    send_ref[...] = dot(hot_ref[...], part_ref[...]).astype(BF).reshape(send_ref.shape)


def pick(pieces, hot, npart):
    count, rank = pieces[0].shape
    return call(
        pick_kernel,
        "pick",
        (
            jax.ShapeDtypeStruct((4 * count, rank), BF),
            jax.ShapeDtypeStruct((npart, CAP, rank), BF),
        ),
        [VMEM] * 5,
        [],
        16,
        2 * hot.size * rank,
        2 * hot.size,
    )(*pieces, hot)


def fold_kernel(expand_ref, l2l_ref, out_ref, wide_ref):
    width, nkids, _ = l2l_ref.shape
    expand = expand_ref[...].astype(F32).T.astype(BF)
    for i, base in enumerate(range(0, width, 128)):
        size = min(128, width - base)
        block = l2l_ref[:, :, base:base + size].astype(F32)
        for p in range(width):
            wide_ref[i, p * PITCH:p * PITCH + nkids, :size] = block[p]
    for c in range(nkids):
        out_ref[c] = dot(expand, kid_rows(wide_ref, c, width, width)).astype(BF)


def fold(expand_t, l2l):
    width, nkids, _ = l2l.shape
    rank = expand_t.shape[1]
    return call(
        fold_kernel,
        "fold",
        jax.ShapeDtypeStruct((nkids, rank, width), BF),
        [VMEM] * 2,
        [pltpu.VMEM((-(-width // 128), (width + 2) * PITCH, 128), F32)],
        24,
        2 * rank * l2l.size,
        2 * l2l.size,
    )(expand_t, l2l)


def either(test, both):
    rank = both.shape[1] // 2
    return jnp.where(test != 0, both[:, rank:].astype(BF), both[:, :rank].astype(BF))


def accumulate(wide_ref, first, table_ref, core_ref, acc_ref, z_ref=None):
    offsets, rank = core_ref.shape[0], core_ref.shape[1]
    table = table_ref[...]
    lane = lax.broadcasted_iota(I32, (1, 128), 1)
    owner = lax.shift_right_logical(lane, 4).astype(I16)
    wanted = ((lane & (SURE - 1)) + 4 * HALF).astype(I16)
    per = 128 // SURE
    mixed, hots = None, []
    for k in range(0, offsets, STEP):
        n = min(STEP, offsets - k)
        lhs = []
        for i in range(k, k + n):
            code = jnp.broadcast_to(wide_ref[:, i:i + 1], wide_ref.shape).astype(I16)
            both = dot(one_hot(code & I16(~HALF), HALF, first), table)
            lhs.append(either(code & I16(HALF), both))
            if z_ref is None:
                continue
            mixed = code if i % per == 0 else jnp.where(owner == I16(i % per), code, mixed)
            if i % per == per - 1 or i == offsets - 1:
                hots.append(jnp.where(mixed == wanted, BF(1), BF(0)))
        core = core_ref[k:k + n].reshape(n * rank, rank)
        acc_ref[...] += dot(jnp.concatenate(lhs, axis=1), core)
        if len(hots) == 2 or (hots and k + n == offsets):
            rows = pl.ds((k + n - 1) // (2 * per) * 256, 128 * len(hots))
            acc_ref[...] += dot(jnp.concatenate(hots, axis=1), z_ref[rows, :])
            hots = []


def widen(code_ref, wide_ref, shifts):
    share = code_ref.shape[0] // 4
    for i, shift in enumerate(shifts):
        start = lax.rem(lax.axis_index("sub") + shift, 4) * share
        rows = code_ref[pl.ds(pl.multiple_of(start, share), share), :]
        wide_ref[i * share:(i + 1) * share, :] = rows.astype(I32)


def near_kernel(code_ref, part_ref, core_ref, acc_ref, table_ref, wide_ref):
    widen(code_ref, wide_ref, range(4))
    rank = part_ref.shape[1]
    table_ref[:, :rank] = part_ref[:HALF, :]
    table_ref[:, rank:] = part_ref[HALF:, :]
    acc_ref[...] = jnp.zeros_like(acc_ref)
    accumulate(wide_ref, 0, table_ref, core_ref, acc_ref)


def near(code, part, core):
    count, rank = part.shape
    return call(
        near_kernel,
        "near",
        jax.ShapeDtypeStruct((count, rank), F32),
        [VMEM] * 3,
        [pltpu.VMEM((HALF, 2 * rank), BF), pltpu.VMEM(code.shape, I32)],
        24,
        2 * count * core.shape[0] * rank * (count + rank),
        2 * core.size,
    )(code, part, core)


def far_kernel(shifts, code_ref, near_ref, got_ref, core_ref, *rest):
    outs, (table_ref, wide_ref, acc_ref, z_ref) = rest[:len(shifts)], rest[len(shifts):]
    widen(code_ref, wide_ref, shifts)
    here = lax.axis_index("dom")
    npart, _, rank = got_ref.shape
    offsets = core_ref.shape[0]
    cut = npart // 2
    table_ref[:, :rank] = got_ref[:cut, :SURE, :].reshape(HALF, rank)
    table_ref[:, rank:] = got_ref[cut:, :SURE, :].reshape(HALF, rank)
    low = got_ref[pl.ds(jnp.maximum(here - 1, 0), 1), SURE:, :].reshape(SURE, rank)
    spot = pl.ds(pl.multiple_of(lax.rem(here, cut) * SURE, SURE), SURE)
    table_ref[spot, :rank] = jnp.where(here < cut, low, table_ref[spot, :rank])
    table_ref[spot, rank:] = jnp.where(here < cut, table_ref[spot, rank:], low)
    high = got_ref[pl.ds(jnp.minimum(here + 1, npart - 1), 1), SURE:, :].reshape(SURE, rank)
    none = jnp.zeros_like(high)
    tail = jnp.concatenate(
        [
            jnp.concatenate([none] * i + [high] + [none] * (STEP - 1 - i), axis=1)
            for i in range(STEP)
        ],
        axis=0,
    )
    zrows = z_ref.shape[0]
    z_ref[offsets * SURE:, :] = jnp.zeros((zrows - offsets * SURE, rank), BF)
    for k in range(0, offsets, STEP):
        n = min(STEP, offsets - k)
        core = core_ref[k:k + n].reshape(n * rank, rank)
        z_ref[k * SURE:(k + n) * SURE, :] = dot(tail[:n * SURE, :n * rank], core).astype(BF)
    share = code_ref.shape[0] // 4
    for i, shift in enumerate(shifts):
        acc_ref[i * share:(i + 1) * share, :] = near_ref[shift * share:(shift + 1) * share, :]
    accumulate(wide_ref, 2 * HALF, table_ref, core_ref, acc_ref, z_ref)
    for i, out in enumerate(outs):
        out[...] = acc_ref[i * share:(i + 1) * share, :].astype(out.dtype)


def far(code, near_sums, got, core, shifts):
    rank = near_sums.shape[1]
    share = near_sums.shape[0] // 4
    count = share * len(shifts)
    offsets = core.shape[0]
    zrows = (offsets * SURE // 128 + 1) * 128
    return call(
        functools.partial(far_kernel, shifts),
        "far",
        tuple(jax.ShapeDtypeStruct((share, rank), BF if shift else F32) for shift in shifts),
        [VMEM] * 4,
        [
            pltpu.VMEM((HALF, 2 * rank), BF),
            pltpu.VMEM((count, 128), I32),
            pltpu.VMEM((count, rank), F32),
            pltpu.VMEM((zrows, rank), BF),
        ],
        24,
        2 * count * offsets * rank * (4 * share + rank),
        2 * core.size,
    )(code, near_sums, got, core)


def down_kernel(own_ref, one_ref, two_ref, three_ref, fold_ref, inh_ref, out_ref, rows_ref):
    nkids, _, width = fold_ref.shape
    count = own_ref.shape[0]
    acc = own_ref[...]
    for ref in (one_ref, two_ref, three_ref):
        acc = acc + ref[...].astype(F32)
    acc = acc.astype(BF)
    for c in range(nkids):
        kid = dot(acc, fold_ref[c])
        kid = jnp.concatenate([kid, jnp.zeros((count, -width % 128), F32)], axis=1)
        for i in range(rows_ref.shape[0]):
            rows_ref[i, pl.ds(c, count, stride=PITCH), :] = kid[:, i * 128:(i + 1) * 128]
    for i, base in enumerate(range(0, width, 128)):
        rows = slice(base, min(base + 128, width))
        for j in range(out_ref.shape[1] // 128):
            cols = slice(j * 128, (j + 1) * 128)
            first = j * 128 // nkids
            far = jnp.concatenate(
                [
                    rows_ref[i, o * PITCH:o * PITCH + nkids, :]
                    for o in range(first, first + 128 // nkids)
                ],
                axis=0,
            ).T[:rows.stop - base]
            out_ref[rows, cols] = (far + inh_ref[rows, cols].astype(F32)).astype(BF)


def downward(pieces, folded, inherited_t):
    nkids, rank, width = folded.shape
    blocks = -(-width // 128)
    return call(
        down_kernel,
        "downward",
        jax.ShapeDtypeStruct(inherited_t.shape, BF),
        [VMEM] * 6,
        [pltpu.VMEM((blocks, (pieces[0].shape[0] + 2) * PITCH, 128), F32)],
        32,
        2 * inherited_t.size * rank,
        2 * (2 * inherited_t.size + folded.size),
    )(*pieces, folded, inherited_t)


def local(leaf_mult, m2m, compress, m2l_core, expand, l2l, inherited, send_rows, m2l_list):
    npart, nsub = lax.axis_size("dom"), lax.axis_size("sub")

    def shifted(x, shift):
        return lax.ppermute(x, "sub", [(i, (i + shift) % nsub) for i in range(nsub)])

    packed = upward(leaf_mult.T, m2m, compress)
    moved = [shifted(packed, shift) for shift in (1, 2, 3)]
    code, hot, own = prepare(m2l_list.T, send_rows.reshape(npart * CAP, 1), packed)
    folded = fold(expand.T, l2l)
    part, send = pick([own] + moved, hot, npart)
    got = lax.all_to_all(send, "dom", 0, 0, tiled=True)
    near_sums = near(code, part, m2l_core)
    order = (0, 2, 1, 3)
    sums = far(code, near_sums, got, m2l_core, order)
    sums = [shifted(x, shift) if shift else x for x, shift in zip(sums, order)]
    return downward(sums, folded, inherited.T).T


def solution(mesh):
    placed = (
        P(("dom", "sub"), None),
        P(),
        P(),
        P("sub", None, None),
        P(),
        P(),
        P(("dom", "sub"), None),
        P("dom", None, None),
        P("dom", "sub"),
    )
    return jax.shard_map(
        local, mesh=mesh, in_specs=placed, out_specs=P(("dom", "sub"), None), check_vma=False
    )
```

```python
import functools

import jax
import jax.numpy as jnp
from jax import lax
from jax.experimental import pallas as pl
from jax.experimental.pallas import tpu as pltpu
from jax.sharding import PartitionSpec as P

BF = jnp.bfloat16
F32 = jnp.float32
I32 = jnp.int32
I16 = jnp.int16
MIB = 1 << 20
CAP = 32
SURE = 16
STEP = 4
HALF = 256
PITCH = 9

VMEM = pl.BlockSpec(memory_space=pltpu.VMEM)
HBM = pl.BlockSpec(memory_space=pltpu.HBM)


def dot(a, b):
    return jnp.dot(a, b, preferred_element_type=F32)


def call(kernel, name, out, ins, scratch, limit, flops, nbytes):
    return pl.pallas_call(
        kernel,
        name=name,
        out_shape=out,
        in_specs=ins,
        out_specs=jax.tree.map(lambda _: VMEM, out),
        scratch_shapes=scratch,
        compiler_params=pltpu.CompilerParams(vmem_limit_bytes=limit * MIB),
        cost_estimate=pl.CostEstimate(flops=flops, bytes_accessed=nbytes, transcendentals=0),
    )


def kid_rows(ref, kid, count, width):
    parts = [ref[i, pl.ds(kid, count, stride=PITCH), :] for i in range(ref.shape[0])]
    return jnp.concatenate(parts, axis=1)[:, :width].astype(BF)


def up_kernel(leaf_ref, m2m_ref, compress_ref, out_ref, leaf_buf, m2m_buf, compress_buf, rows_ref, sems):
    nkids, width = m2m_ref.shape[0], m2m_ref.shape[1]
    count = leaf_ref.shape[1] // nkids
    first = pltpu.make_async_copy(leaf_ref, leaf_buf, sems.at[nkids])
    copies = [
        pltpu.make_async_copy(m2m_ref.at[c], m2m_buf.at[c], sems.at[c]) for c in range(nkids)
    ]
    last = pltpu.make_async_copy(compress_ref, compress_buf, sems.at[nkids + 1])
    first.start()
    for copy in copies:
        copy.start()
    last.start()
    first.wait()
    for j in range(leaf_ref.shape[1] // 128):
        cols = slice(j * 128, (j + 1) * 128)
        for i, base in enumerate(range(0, width, 128)):
            size = min(128, width - base)
            turned = leaf_buf[base:base + size, cols].astype(F32).T
            for o in range(0, 128, nkids):
                at = (j * 128 + o) // nkids * PITCH
                rows_ref[i, at:at + nkids, :size] = turned[o:o + nkids]
    total = jnp.zeros((count, width), F32)
    for c in range(nkids):
        kid = kid_rows(rows_ref, c, count, width)
        copies[c].wait()
        total = total + dot(kid, m2m_buf[c])
    last.wait()
    out_ref[...] = dot(total.astype(BF), compress_buf[...]).astype(BF)


def upward(leaf_t, m2m, compress):
    nkids, width, _ = m2m.shape
    count = leaf_t.shape[1] // nkids
    return call(
        up_kernel,
        "upward",
        jax.ShapeDtypeStruct((count, compress.shape[1]), BF),
        [HBM] * 3,
        [
            pltpu.VMEM(leaf_t.shape, BF),
            pltpu.VMEM(m2m.shape, BF),
            pltpu.VMEM(compress.shape, BF),
            pltpu.VMEM((-(-width // 128), (count + 2) * PITCH, 128), F32),
            pltpu.SemaphoreType.DMA((nkids + 2,)),
        ],
        60,
        2 * leaf_t.size * width,
        2 * (leaf_t.size + m2m.size),
    )(leaf_t, m2m, compress)


def one_hot(row, depth, first=0):
    lane = lax.broadcasted_iota(I32, (1, 128), 1)
    return jnp.concatenate(
        [
            jnp.where(row == (lane + (first + base)).astype(I16), BF(1), BF(0))
            for base in range(0, depth, 128)
        ],
        axis=1,
    )


def neighbours(part, npart):
    return jnp.maximum(part - 1, 0), jnp.minimum(part + 1, npart - 1)


def prep_kernel(list_ref, rows_ref, packed_ref, code_ref, hot_ref, own_ref):
    own_ref[...] = packed_ref[...]
    part = lax.axis_index("dom")
    offsets, count = list_ref.shape
    npart = rows_ref.shape[0] // CAP
    rows = [rows_ref[p * CAP:p * CAP + SURE, :] for p in range(npart)]
    for side in neighbours(part, npart):
        rows.append(rows_ref[pl.ds(pl.multiple_of(side * CAP + SURE, SURE), SURE), :])
    rows = jnp.concatenate(rows, axis=0)
    hot_ref[...] = one_hot(jnp.broadcast_to(rows, (rows.shape[0], 128)).astype(I16), count)
    value = list_ref[...]
    source = lax.shift_right_arithmetic(value - count, 5)
    slot = value & (CAP - 1)
    sure = slot < SURE
    row = jnp.where(sure, source * SURE + slot, part * SURE + slot - SURE)
    extra = ~sure & (source > part)
    code = jnp.where(extra, slot + (2 * count - SURE), row + count)
    code = jnp.where(value < count, value, code)
    code = jnp.concatenate([code, jnp.full((128 - offsets, count), -1, I32)], axis=0)
    for j in range(count // 128):
        cols = slice(j * 128, (j + 1) * 128)
        code_ref[cols, :] = code[:, cols].T.astype(I16)


def prepare(list_t, rows, packed):
    count = list_t.shape[1]
    return call(
        prep_kernel,
        "prepare",
        (
            jax.ShapeDtypeStruct((count, 128), I16),
            jax.ShapeDtypeStruct(((rows.shape[0] // CAP + 2) * SURE, count), BF),
            jax.ShapeDtypeStruct(packed.shape, BF),
        ),
        [VMEM] * 3,
        [],
        16,
        1,
        4 * list_t.size,
    )(list_t, rows, packed)


def pick_kernel(own_ref, one_ref, two_ref, three_ref, hot_ref, part_ref, send_ref):
    me = lax.axis_index("sub")
    count = own_ref.shape[0]
    for shift, ref in enumerate((own_ref, one_ref, two_ref, three_ref)):
        start = lax.rem(me + (4 - shift), 4) * count
        part_ref[pl.ds(pl.multiple_of(start, count), count), :] = ref[...]
    npart, _, rank = send_ref.shape
    rows = dot(hot_ref[...], part_ref[...]).astype(BF).reshape(npart + 2, SURE, rank)
    send_ref[:, :SURE, :] = rows[:npart]
    send_ref[:, SURE:, :] = jnp.zeros((npart, CAP - SURE, rank), BF)
    for i, side in enumerate(neighbours(lax.axis_index("dom"), npart)):
        send_ref[pl.ds(side, 1), SURE:, :] = rows[npart + i:npart + i + 1]


def pick(pieces, hot, npart):
    count, rank = pieces[0].shape
    return call(
        pick_kernel,
        "pick",
        (
            jax.ShapeDtypeStruct((4 * count, rank), BF),
            jax.ShapeDtypeStruct((npart, CAP, rank), BF),
        ),
        [VMEM] * 5,
        [],
        16,
        2 * hot.size * rank,
        2 * hot.size,
    )(*pieces, hot)


def fold_kernel(expand_ref, l2l_ref, out_ref, wide_ref):
    width, nkids, _ = l2l_ref.shape
    expand = expand_ref[...].astype(F32).T.astype(BF)
    for i, base in enumerate(range(0, width, 128)):
        size = min(128, width - base)
        block = l2l_ref[:, :, base:base + size].astype(F32)
        for p in range(width):
            wide_ref[i, p * PITCH:p * PITCH + nkids, :size] = block[p]
    for c in range(nkids):
        out_ref[c] = dot(expand, kid_rows(wide_ref, c, width, width)).astype(BF)


def fold(expand_t, l2l):
    width, nkids, _ = l2l.shape
    rank = expand_t.shape[1]
    return call(
        fold_kernel,
        "fold",
        jax.ShapeDtypeStruct((nkids, rank, width), BF),
        [VMEM] * 2,
        [pltpu.VMEM((-(-width // 128), (width + 2) * PITCH, 128), F32)],
        24,
        2 * rank * l2l.size,
        2 * l2l.size,
    )(expand_t, l2l)


def either(test, both):
    rank = both.shape[1] // 2
    return jnp.where(test != 0, both[:, rank:].astype(BF), both[:, :rank].astype(BF))


def accumulate(wide_ref, first, table_ref, core_ref, acc_ref, z_ref=None):
    offsets, rank = core_ref.shape[0], core_ref.shape[1]
    table = table_ref[...]
    lane = lax.broadcasted_iota(I32, (1, 128), 1)
    owner = lax.shift_right_logical(lane, 4).astype(I16)
    wanted = ((lane & (SURE - 1)) + 4 * HALF).astype(I16)
    per = 128 // SURE
    mixed, hots = None, []
    for k in range(0, offsets, STEP):
        n = min(STEP, offsets - k)
        lhs = []
        for i in range(k, k + n):
            code = jnp.broadcast_to(wide_ref[:, i:i + 1], wide_ref.shape).astype(I16)
            both = dot(one_hot(code & I16(~HALF), HALF, first), table)
            lhs.append(either(code & I16(HALF), both))
            if z_ref is None:
                continue
            mixed = code if i % per == 0 else jnp.where(owner == I16(i % per), code, mixed)
            if i % per == per - 1 or i == offsets - 1:
                hots.append(jnp.where(mixed == wanted, BF(1), BF(0)))
        core = core_ref[k:k + n].reshape(n * rank, rank)
        acc_ref[...] += dot(jnp.concatenate(lhs, axis=1), core)
        if len(hots) == 2 or (hots and k + n == offsets):
            rows = pl.ds((k + n - 1) // (2 * per) * 256, 128 * len(hots))
            acc_ref[...] += dot(jnp.concatenate(hots, axis=1), z_ref[rows, :])
            hots = []


def widen(code_ref, wide_ref, shifts):
    share = code_ref.shape[0] // 4
    for i, shift in enumerate(shifts):
        start = lax.rem(lax.axis_index("sub") + shift, 4) * share
        rows = code_ref[pl.ds(pl.multiple_of(start, share), share), :]
        wide_ref[i * share:(i + 1) * share, :] = rows.astype(I32)


def near_kernel(code_ref, part_ref, core_ref, acc_ref, table_ref, wide_ref):
    widen(code_ref, wide_ref, range(4))
    rank = part_ref.shape[1]
    table_ref[:, :rank] = part_ref[:HALF, :]
    table_ref[:, rank:] = part_ref[HALF:, :]
    acc_ref[...] = jnp.zeros_like(acc_ref)
    accumulate(wide_ref, 0, table_ref, core_ref, acc_ref)


def near(code, part, core):
    count, rank = part.shape
    return call(
        near_kernel,
        "near",
        jax.ShapeDtypeStruct((count, rank), F32),
        [VMEM] * 3,
        [pltpu.VMEM((HALF, 2 * rank), BF), pltpu.VMEM(code.shape, I32)],
        24,
        2 * count * core.shape[0] * rank * (count + rank),
        2 * core.size,
    )(code, part, core)


def far_kernel(shifts, code_ref, near_ref, got_ref, core_ref, *rest):
    outs, (table_ref, wide_ref, acc_ref, z_ref) = rest[:len(shifts)], rest[len(shifts):]
    widen(code_ref, wide_ref, shifts)
    here = lax.axis_index("dom")
    npart, _, rank = got_ref.shape
    offsets = core_ref.shape[0]
    cut = npart // 2
    table_ref[:, :rank] = got_ref[:cut, :SURE, :].reshape(HALF, rank)
    table_ref[:, rank:] = got_ref[cut:, :SURE, :].reshape(HALF, rank)
    low = got_ref[pl.ds(jnp.maximum(here - 1, 0), 1), SURE:, :].reshape(SURE, rank)
    spot = pl.ds(pl.multiple_of(lax.rem(here, cut) * SURE, SURE), SURE)
    table_ref[spot, :rank] = jnp.where(here < cut, low, table_ref[spot, :rank])
    table_ref[spot, rank:] = jnp.where(here < cut, table_ref[spot, rank:], low)
    high = got_ref[pl.ds(jnp.minimum(here + 1, npart - 1), 1), SURE:, :].reshape(SURE, rank)
    none = jnp.zeros_like(high)
    tail = jnp.concatenate(
        [
            jnp.concatenate([none] * i + [high] + [none] * (STEP - 1 - i), axis=1)
            for i in range(STEP)
        ],
        axis=0,
    )
    zrows = z_ref.shape[0]
    z_ref[offsets * SURE:, :] = jnp.zeros((zrows - offsets * SURE, rank), BF)
    for k in range(0, offsets, STEP):
        n = min(STEP, offsets - k)
        core = core_ref[k:k + n].reshape(n * rank, rank)
        z_ref[k * SURE:(k + n) * SURE, :] = dot(tail[:n * SURE, :n * rank], core).astype(BF)
    share = code_ref.shape[0] // 4
    for i, shift in enumerate(shifts):
        acc_ref[i * share:(i + 1) * share, :] = near_ref[shift * share:(shift + 1) * share, :]
    accumulate(wide_ref, 2 * HALF, table_ref, core_ref, acc_ref, z_ref)
    for i, out in enumerate(outs):
        out[...] = acc_ref[i * share:(i + 1) * share, :].astype(out.dtype)


def far(code, near_sums, got, core, shifts):
    rank = near_sums.shape[1]
    share = near_sums.shape[0] // 4
    count = share * len(shifts)
    offsets = core.shape[0]
    zrows = (offsets * SURE // 128 + 1) * 128
    return call(
        functools.partial(far_kernel, shifts),
        "far",
        tuple(jax.ShapeDtypeStruct((share, rank), BF if shift else F32) for shift in shifts),
        [VMEM] * 4,
        [
            pltpu.VMEM((HALF, 2 * rank), BF),
            pltpu.VMEM((count, 128), I32),
            pltpu.VMEM((count, rank), F32),
            pltpu.VMEM((zrows, rank), BF),
        ],
        24,
        2 * count * offsets * rank * (4 * share + rank),
        2 * core.size,
    )(code, near_sums, got, core)


def down_kernel(own_ref, one_ref, two_ref, three_ref, fold_ref, inh_ref, out_ref, rows_ref):
    nkids, _, width = fold_ref.shape
    count = own_ref.shape[0]
    acc = own_ref[...]
    for ref in (one_ref, two_ref, three_ref):
        acc = acc + ref[...].astype(F32)
    acc = acc.astype(BF)
    for c in range(nkids):
        kid = dot(acc, fold_ref[c])
        kid = jnp.concatenate([kid, jnp.zeros((count, -width % 128), F32)], axis=1)
        for i in range(rows_ref.shape[0]):
            rows_ref[i, pl.ds(c, count, stride=PITCH), :] = kid[:, i * 128:(i + 1) * 128]
    for i, base in enumerate(range(0, width, 128)):
        rows = slice(base, min(base + 128, width))
        for j in range(out_ref.shape[1] // 128):
            cols = slice(j * 128, (j + 1) * 128)
            first = j * 128 // nkids
            far = jnp.concatenate(
                [
                    rows_ref[i, o * PITCH:o * PITCH + nkids, :]
                    for o in range(first, first + 128 // nkids)
                ],
                axis=0,
            ).T[:rows.stop - base]
            out_ref[rows, cols] = (far + inh_ref[rows, cols].astype(F32)).astype(BF)


def downward(pieces, folded, inherited_t):
    nkids, rank, width = folded.shape
    blocks = -(-width // 128)
    return call(
        down_kernel,
        "downward",
        jax.ShapeDtypeStruct(inherited_t.shape, BF),
        [VMEM] * 6,
        [pltpu.VMEM((blocks, (pieces[0].shape[0] + 2) * PITCH, 128), F32)],
        32,
        2 * inherited_t.size * rank,
        2 * (2 * inherited_t.size + folded.size),
    )(*pieces, folded, inherited_t)


def local(leaf_mult, m2m, compress, m2l_core, expand, l2l, inherited, send_rows, m2l_list):
    npart, nsub = lax.axis_size("dom"), lax.axis_size("sub")

    def shifted(x, shift):
        return lax.ppermute(x, "sub", [(i, (i + shift) % nsub) for i in range(nsub)])

    packed = upward(leaf_mult.T, m2m, compress)
    moved = [shifted(packed, shift) for shift in (1, 2, 3)]
    code, hot, own = prepare(m2l_list.T, send_rows.reshape(npart * CAP, 1), packed)
    folded = fold(expand.T, l2l)
    part, send = pick([own] + moved, hot, npart)
    got = lax.all_to_all(send, "dom", 0, 0, tiled=True)
    near_sums = near(code, part, m2l_core)
    sums = far(code, near_sums, got, m2l_core, (0, 1, 2, 3))
    sums = [sums[0]] + [shifted(sums[shift], shift) for shift in (1, 2, 3)]
    return downward(sums, folded, inherited.T).T


def solution(mesh):
    placed = (
        P(("dom", "sub"), None),
        P(),
        P(),
        P("sub", None, None),
        P(),
        P(),
        P(("dom", "sub"), None),
        P("dom", None, None),
        P("dom", "sub"),
    )
    return jax.shard_map(
        local, mesh=mesh, in_specs=placed, out_specs=P(("dom", "sub"), None), check_vma=False
    )
```
